32 devices in a mesh: sens: 2 (over core), pts: 16 (over z, y, x).
Axes of the slice: x: 2, y: 2, z: 4, core: 2. Of those that a mesh axis runs over, the one named last changes fastest.
Arguments:
- kernel: float32 [16, 1024, 384], P('sens', 'pts'), may hold values from -0.009765625 to 0.009765625
- vectors: float32 [8, 1024, 384], P(None, 'pts'), may hold values from -6 to 6
- noise_scale: float32 [16], P('sens'), may hold values from 0.5 to 2
- sensor_group: int32 [16], P('sens'), may hold values from 0 to 3
- correlation: float32 [4, 384, 384], replicated, may hold values from -0.3125 to 0.3125
- stiffness: float32 [1024], P('pts'), may hold values from 0.2 to 1
- couplings: float32 [4, 1024], P(None, 'pts'), may hold values from 0.05 to 0.5
- neighbors: int32 [4, 1024], P(None, 'pts'), may hold values from 0 to 1023, as said below
Outputs:
- hessian_action: float32 [8, 1024, 384], P('sens', 'pts')
The draws below stay inside these ranges and needn't reach their ends.
Inputs may be any that keep to these rules, and one draw needn't show every extreme that they name: `neighbors`: points are numbered row by row on a grid of rows of 16 points; every neighbor of point p lies in p's grid row or in one of the two rows beside it.
All inputs are finite; a program needn't handle non-finite values.
Results may differ from the reference program's by a relative error of at most 0.0001.
Values sent between devices are 32-bit elements; how exact they have to be, the bound alone decides.
No kernel may reach another device: no remote copies, remote signals or barrier semaphores. Data moves between devices by JAX's collectives and lax.ppermute only.
A program may use at most 64 MiB of HBM per device.

```python
import math
import jax
import jax.numpy as jnp
from jax import lax

K = 8
NT = 384
NB = 4
S_DEV = 8
COLS = 16
S = 16
NP = 1024
N_SENS = 2


def draw_neighbors(key, part):
    grid_rows = NP // COLS
    index = jnp.arange(NP, dtype=jnp.int32)
    row = index // COLS
    column = index % COLS
    jitter = jax.random.randint(jax.random.fold_in(key, 17), (2, NP), -1, 2).astype(jnp.int32)
    upper = jnp.maximum(row - 1, 0) * COLS + jnp.clip(column + jitter[0], 0, COLS - 1)
    lower = jnp.minimum(row + 1, grid_rows - 1) * COLS + jnp.clip(column + jitter[1], 0, COLS - 1)
    left = row * COLS + jnp.maximum(column - 1, 0)
    right = row * COLS + jnp.minimum(column + 1, COLS - 1)
    return jnp.stack([upper, lower, left, right]).astype(jnp.int32)


def touch_ends(result, rng, low, top_value):
    dims = result.shape
    index_at = [jax.random.randint(jax.random.fold_in(rng, axis), (), 0, dims[axis]) for axis in range(len(dims))]
    result = result.at[tuple(index_at)].set(low)
    longest = dims.index(max(dims))
    index_at[longest] = (index_at[longest] + 1) % dims[longest]
    return result.at[tuple(index_at)].set(top_value)


def shard_levels(rng, dims, cuts, smallest, largest):
    factor_of = 1.0
    for position, shards_of in cuts:
        steps = jax.random.uniform(jax.random.fold_in(jax.random.fold_in(rng, 6), position), (shards_of,), jnp.float32, smallest / len(cuts), largest / len(cuts))
        factor_of = factor_of * jnp.repeat(jnp.exp(steps), dims[position] // shards_of).reshape((-1,) + (1,) * (len(dims) - 1 - position))
    return factor_of


def centred(own_key, dims, spread, most, cuts=(), held_as=jnp.bfloat16):
    values = spread * jax.random.normal(own_key, dims, jnp.float32)
    if cuts:
        values = values * shard_levels(own_key, dims, cuts, -0.22, 0.18)
    return jnp.clip(values, -most, most).astype(held_as)


def setup_inputs(seed: int = 0) -> dict:
    keys = jax.random.split(jax.random.key(seed), 9)
    kernel = centred(keys[0], (S, NP, NT), (NP * NT) ** -0.5, 0.009765625, ((0, 2), (1, 16)), jnp.float32)
    vectors = centred(keys[1], (K, NP, NT), 1.0, 6.0, ((1, 16),), jnp.float32)
    noise_scale = jnp.clip(jnp.exp(math.log(2.0) - 1.3862944 * jax.random.uniform(keys[2], (S,), jnp.float32) ** shard_levels(keys[2], (S,), ((0, 2),), -0.2, 0.2)), 0.5, 2.0)
    sensor_group = touch_ends(jax.random.randint(keys[3], (S,), 0, NB), jax.random.fold_in(keys[3], 1), 0, NB - 1).astype(jnp.int32)
    correlation = centred(keys[4], (NB, NT, NT), NT ** -0.5, 0.3125, (), jnp.float32)
    stiffness = jnp.clip(jnp.exp(math.log(1.0) - 1.609438 * jax.random.uniform(keys[5], (NP,), jnp.float32) ** shard_levels(keys[5], (NP,), ((0, 16),), -0.2, 0.2)), 0.2, 1.0)
    couplings = jnp.clip(jnp.exp(math.log(0.5) - 2.3025851 * jax.random.uniform(keys[6], (4, NP), jnp.float32) ** shard_levels(keys[6], (4, NP), ((1, 16),), -0.2, 0.2)), 0.05, 0.5)
    neighbors = draw_neighbors(jax.random.fold_in(keys[8], 71), 0)
    return dict(kernel=kernel, vectors=vectors, noise_scale=noise_scale, sensor_group=sensor_group, correlation=correlation, stiffness=stiffness, couplings=couplings, neighbors=neighbors)


def reference(kernel, vectors, noise_scale, sensor_group, correlation, stiffness, couplings, neighbors):
    span = 2 * NT
    vec_hat = jnp.fft.rfft(vectors, n=span, axis=-1)
    blocks = kernel.reshape(N_SENS, S_DEV, NP, NT)

    def forward_block(block):
        kern_hat = jnp.fft.rfft(block, n=span, axis=-1)
        pred_hat = jnp.einsum('kpf,spf->ksf', vec_hat, kern_hat)
        return jnp.fft.irfft(pred_hat, n=span, axis=-1)[..., :NT]

    predicted = lax.map(forward_block, blocks)
    predicted = jnp.transpose(predicted, (1, 0, 2, 3)).reshape(K, S, NT)
    corr_sensor = correlation[sensor_group]
    mixed = jnp.einsum('sut,kst->ksu', corr_sensor, predicted, precision=lax.Precision.HIGHEST)
    residual = noise_scale[None, :, None] * (predicted + mixed)
    res_blocks = jnp.transpose(residual.reshape(K, N_SENS, S_DEV, NT), (1, 0, 2, 3))

    def adjoint(total, pair):
        block, res = pair
        kern_hat = jnp.fft.rfft(block, n=span, axis=-1)
        res_hat = jnp.fft.rfft(res, n=span, axis=-1)
        return total + jnp.einsum('ksf,spf->kpf', res_hat, jnp.conj(kern_hat)), None

    start = jnp.zeros(vec_hat.shape, vec_hat.dtype)
    grad_hat, _ = lax.scan(adjoint, start, (blocks, res_blocks))
    data_term = jnp.fft.irfft(grad_hat, n=span, axis=-1)[..., :NT]
    gathered = vectors[:, neighbors]
    prior_term = stiffness[None, :, None] * vectors
    prior_term = prior_term + jnp.sum(couplings[None, :, :, None] * (vectors[:, None] - gathered), axis=1)
    return data_term + prior_term
```

```python
import functools
import math

import jax
import jax.numpy as jnp
import ml_dtypes
import numpy as np
from jax import lax
from jax.experimental import pallas as pl
from jax.experimental.pallas import tpu as pltpu
from jax.sharding import PartitionSpec as P

COLS = 16
LANES = 128
SUB = 8
F32 = jnp.float32
BF16 = jnp.bfloat16
NT_DIMS = (((1,), (1,)), ((), ()))


def dft_table(length):
    steps = np.arange(length, dtype=np.int64)
    phase = (steps[:, None] * (2 * steps[None, :] + 1)) % (4 * length)
    angle = phase.astype(np.float64) * (2.0 * math.pi / (4 * length))
    table = np.concatenate([np.cos(angle), -np.sin(angle)], axis=1)
    high = table.astype(ml_dtypes.bfloat16)
    low = (table - high.astype(np.float64)).astype(ml_dtypes.bfloat16)
    return np.concatenate([high, low], axis=0)


def split(x):
    high = x.astype(BF16)
    return high, (x - high.astype(F32)).astype(BF16)


def dot(a, b):
    return jnp.dot(a, b, preferred_element_type=F32)


def dot_nt(a, b):
    return lax.dot_general(a, b, NT_DIMS, preferred_element_type=F32)


def dft(high, low, table_ref, length):
    return dot(high, table_ref[:length]) + dot(high, table_ref[length:]) + dot(low, table_ref[:length])


def inverse_dft(high, low, table_ref, length):
    return (
        dot_nt(high, table_ref[:length])
        + dot_nt(high, table_ref[length:])
        + dot_nt(low, table_ref[:length])
    )


def forward_kernel(
    shift_ref, kern_ref, vec_ref, table_ref, pred_ref, khat_ref, vhat_ref, high_ref, low_ref, spec_ref
):
    sensors, points, length = kern_ref.shape
    count = vec_ref.shape[0]
    shift = shift_ref[0]
    cols = length // LANES

    def load_kern(s, _):
        rows = pl.ds(pl.multiple_of(s * points, points), points)
        high_ref[rows], low_ref[rows] = split(kern_ref[s])
        return 0

    def load_vec(k, _):
        rows = pl.ds(pl.multiple_of(k * points, points), points)
        high_ref[rows], low_ref[rows] = split(vec_ref[lax.rem(k + shift, count)])
        return 0

    lax.fori_loop(0, sensors, load_kern, 0)
    rows = sensors * points
    hat = dft(high_ref[:rows], low_ref[:rows], table_ref, length)
    real, imag = hat[:, :length], hat[:, length:]
    khat_ref[0] = real
    khat_ref[1] = imag - real
    khat_ref[2] = imag + real

    lax.fori_loop(0, count, load_vec, 0)
    rows = count * points
    hat = dft(high_ref[:rows], low_ref[:rows], table_ref, length)
    real, imag = hat[:, :length], hat[:, length:]
    vhat_ref[0] = real + imag
    vhat_ref[1] = real
    vhat_ref[2] = imag

    k_block, s_block = 2, sensors // 2
    sub_iota = lax.broadcasted_iota(jnp.int32, (sensors, LANES), 0)

    def product(step, _):
        k0 = step // cols * k_block
        lanes = pl.ds(pl.multiple_of(step % cols * LANES, LANES), LANES)
        out_re = [jnp.zeros((sensors, LANES), F32) for _ in range(k_block)]
        out_im = [jnp.zeros((sensors, LANES), F32) for _ in range(k_block)]
        for s0 in range(0, sensors, s_block):
            acc = [[[None] * 3 for _ in range(s_block)] for _ in range(k_block)]
            for g in range(points // SUB):
                left = [
                    [
                        vhat_ref[c, pl.ds(pl.multiple_of((k0 + i) * points + g * SUB, SUB), SUB), lanes]
                        for c in range(3)
                    ]
                    for i in range(k_block)
                ]
                for j in range(s_block):
                    right = [
                        khat_ref[c, pl.ds((s0 + j) * points + g * SUB, SUB), lanes] for c in range(3)
                    ]
                    for i in range(k_block):
                        for c in range(3):
                            term = left[i][c] * right[c]
                            acc[i][j][c] = term if acc[i][j][c] is None else acc[i][j][c] + term
            for i in range(k_block):
                for j in range(s_block):
                    one, two, three = acc[i][j]
                    re = jnp.sum(one - three, axis=0, keepdims=True)
                    im = jnp.sum(one + two, axis=0, keepdims=True)
                    out_re[i] = jnp.where(sub_iota == s0 + j, re, out_re[i])
                    out_im[i] = jnp.where(sub_iota == s0 + j, im, out_im[i])
        for i in range(k_block):
            at = pl.ds(pl.multiple_of((k0 + i) * sensors, sensors), sensors)
            spec_ref[at, lanes] = out_re[i]
            other = pl.ds(pl.multiple_of(step % cols * LANES + length, LANES), LANES)
            spec_ref[at, other] = out_im[i]
        return 0

    lax.fori_loop(0, count // k_block * cols, product, 0)
    high, low = split(spec_ref[...])
    pred_ref[...] = inverse_dft(high, low, table_ref, length) * (1.0 / length)


def forward(shift, kernel, vectors, table):
    sensors, points, length = kernel.shape
    count = vectors.shape[0]
    most = max(sensors, count) * points
    vmem = pl.BlockSpec(memory_space=pltpu.VMEM)
    smem = pl.BlockSpec(memory_space=pltpu.SMEM)
    return pl.pallas_call(
        forward_kernel,
        out_shape=(
            jax.ShapeDtypeStruct((count * sensors, length), F32),
            jax.ShapeDtypeStruct((3, sensors * points, length), F32),
        ),
        in_specs=[smem, vmem, vmem, vmem],
        out_specs=(vmem, vmem),
        scratch_shapes=[
            pltpu.VMEM((3, count * points, length), F32),
            pltpu.VMEM((most, length), BF16),
            pltpu.VMEM((most, length), BF16),
            pltpu.VMEM((count * sensors, 2 * length), F32),
        ],
        compiler_params=pltpu.CompilerParams(vmem_limit_bytes=40 * 1024 * 1024),
    )(shift, kernel, vectors, table)


def adjoint_kernel(
    own,
    pred_ref,
    more_ref,
    scale_ref,
    mask_ref,
    corr_ref,
    khat_ref,
    table_ref,
    prior_ref,
    out_ref,
    rest_ref,
    rhat_ref,
    high_ref,
    low_ref,
):
    groups, length, _ = corr_ref.shape
    rows = pred_ref.shape[0]
    count = high_ref.shape[0] // prior_ref.shape[1]
    points = prior_ref.shape[1]
    sensors = rows // count
    cols = length // LANES
    pred = pred_ref[...] + more_ref[...]
    high, low = split(pred)
    mixed = pred
    for g in range(groups):
        corr_high, corr_low = split(corr_ref[g])
        part = dot_nt(high, corr_high) + dot_nt(high, corr_low) + dot_nt(low, corr_high)
        mixed = mixed + mask_ref[:, g : g + 1] * part
    residual = mixed * scale_ref[:, 0:1]
    high, low = split(residual)
    hat = dft(high, low, table_ref, length)
    real, imag = hat[:, :length], hat[:, length:]
    rhat_ref[0] = jnp.broadcast_to((real + imag)[:, None, :], (rows, SUB, length))
    rhat_ref[1] = jnp.broadcast_to(imag[:, None, :], (rows, SUB, length))
    rhat_ref[2] = jnp.broadcast_to(real[:, None, :], (rows, SUB, length))

    k_block, g_block = 4, 2
    tall = g_block * SUB
    blocks = points // tall

    def product(step, _):
        col = step % cols
        g0 = step // cols % blocks
        k0 = step // (cols * blocks) * k_block
        lanes = pl.ds(pl.multiple_of(col * LANES, LANES), LANES)
        others = pl.ds(pl.multiple_of(col * LANES + length, LANES), LANES)
        acc = [[[None] * 3 for _ in range(g_block)] for _ in range(k_block)]
        for s in range(sensors):
            right = [
                [
                    khat_ref[c, pl.ds(pl.multiple_of(g0 * tall, tall) + s * points + b * SUB, SUB), lanes]
                    for c in range(3)
                ]
                for b in range(g_block)
            ]
            for i in range(k_block):
                left = [rhat_ref[c, (k0 + i) * sensors + s, :, lanes] for c in range(3)]
                for b in range(g_block):
                    for c in range(3):
                        term = left[c] * right[b][c]
                        acc[i][b][c] = term if acc[i][b][c] is None else acc[i][b][c] + term
        for i in range(k_block):
            re = jnp.concatenate([one + two for one, two, _ in acc[i]], axis=0)
            im = jnp.concatenate([one - three for one, _, three in acc[i]], axis=0)
            at = pl.ds(pl.multiple_of((k0 + i) * points + g0 * tall, tall), tall)
            high_ref[at, lanes], low_ref[at, lanes] = split(re)
            high_ref[at, others], low_ref[at, others] = split(im)
        return 0

    lax.fori_loop(0, count // k_block * blocks * cols, product, 0)
    data = inverse_dft(high_ref[...], low_ref[...], table_ref, length)
    data = data.reshape(count, points, length)
    out_ref[...] = data[:own] + prior_ref[...]
    rest_ref[...] = data[own:]


def adjoint(pred, more, scale, mask, correlation, khat, table, prior, count):
    rows, length = pred.shape
    own, points, _ = prior.shape
    vmem = pl.BlockSpec(memory_space=pltpu.VMEM)
    return pl.pallas_call(
        functools.partial(adjoint_kernel, own),
        out_shape=(
            jax.ShapeDtypeStruct((own, points, length), F32),
            jax.ShapeDtypeStruct((count - own, points, length), F32),
        ),
        in_specs=[vmem] * 8,
        out_specs=(vmem, vmem),
        scratch_shapes=[
            pltpu.VMEM((3, rows, SUB, length), F32),
            pltpu.VMEM((count * points, 2 * length), BF16),
            pltpu.VMEM((count * points, 2 * length), BF16),
        ],
        compiler_params=pltpu.CompilerParams(vmem_limit_bytes=40 * 1024 * 1024),
    )(pred, more, scale, mask, correlation, khat, table, prior)


def prior_kernel(shift_ref, base_ref, vec_ref, low_ref, high_ref, stiff_ref, coup_ref, near_ref, out_ref):
    own, points, _ = out_ref.shape
    halo = low_ref.shape[1]
    count = vec_ref.shape[0]
    span = points + 2 * halo
    place = lax.broadcasted_iota(jnp.int32, (span, points), 0)
    coup = coup_ref[...]
    here = lax.broadcasted_iota(jnp.int32, (span, points), 1) + halo
    diagonal = stiff_ref[...] + jnp.sum(coup, axis=0, keepdims=True)
    weight = jnp.where(place == here, diagonal, 0.0)
    near = near_ref[...] - base_ref[0]
    for j in range(coup.shape[0]):
        weight = weight - jnp.where(place == near[j : j + 1], coup[j : j + 1], 0.0)
    weight_high, weight_low = split(weight.T)
    for k in range(own):
        value = jnp.concatenate(
            [low_ref[k], vec_ref[lax.rem(shift_ref[0] + k, count)], high_ref[k]], axis=0
        )
        high, low = split(value)
        out_ref[k] = dot(weight_high, high) + dot(weight_high, low) + dot(weight_low, high)


def prior_term(shift, base, vectors, low, high, stiffness, couplings, neighbors):
    own = low.shape[0]
    _, points, length = vectors.shape
    vmem = pl.BlockSpec(memory_space=pltpu.VMEM)
    smem = pl.BlockSpec(memory_space=pltpu.SMEM)
    return pl.pallas_call(
        prior_kernel,
        out_shape=jax.ShapeDtypeStruct((own, points, length), F32),
        in_specs=[smem, smem] + [vmem] * 6,
        out_specs=vmem,
        compiler_params=pltpu.CompilerParams(vmem_limit_bytes=40 * 1024 * 1024),
    )(shift, base, vectors, low, high, stiffness[None], couplings, neighbors)


def butterfly_masks(size):
    masks = [1 << bit for bit in range(size.bit_length() - 1)]
    order = []
    while masks:
        order.append(masks.pop(0))
        if masks:
            order.append(masks.pop())
    swapped = list(order)
    for i in range(0, len(order) - 1, 2):
        swapped[i], swapped[i + 1] = order[i + 1], order[i]
    return order, swapped


def local(table, kernel, vectors, noise_scale, sensor_group, correlation, stiffness, couplings, neighbors):
    sensors, points, length = kernel.shape
    count = vectors.shape[0]
    n_sens, n_pts = lax.axis_size("sens"), lax.axis_size("pts")
    sens, pts = lax.axis_index("sens"), lax.axis_index("pts")
    own = count // n_sens
    shift = (sens * own).reshape(1)

    pred, khat = forward(shift, kernel, vectors, table)

    own_vectors = lax.dynamic_slice_in_dim(vectors, sens * own, own, 0)
    ahead = [(i, i + 1) for i in range(n_pts - 1)]
    behind = [(i + 1, i) for i in range(n_pts - 1)]
    low = lax.ppermute(own_vectors[:, points - COLS :], "pts", ahead)
    high = lax.ppermute(own_vectors[:, :COLS], "pts", behind)
    base = (pts * points - COLS).reshape(1)
    prior = prior_term(shift, base, vectors, low, high, stiffness, couplings, neighbors)

    more = jnp.zeros_like(pred)
    even, odd = butterfly_masks(n_pts)
    for step, (mask_even, mask_odd) in enumerate(zip(even, odd)):
        pairs = [
            (s * n_pts + p, s * n_pts + (p ^ (mask_odd if s % 2 else mask_even)))
            for s in range(n_sens)
            for p in range(n_pts)
        ]
        if step:
            pred = pred + more
        more = lax.ppermute(pred, ("sens", "pts"), pairs)

    row_scale = jnp.tile(noise_scale * (1.0 / length), count)[:, None]
    groups = correlation.shape[0]
    row_mask = (jnp.tile(sensor_group, count)[:, None] == jnp.arange(groups)[None, :]).astype(F32)
    total, rest = adjoint(pred, more, row_scale, row_mask, correlation, khat, table, prior, count)
    for j in range(1, n_sens):
        pairs = [(s, (s + j) % n_sens) for s in range(n_sens)]
        total = total + lax.ppermute(rest[(j - 1) * own : j * own], "sens", pairs)
    return total


def solution(mesh):
    in_specs = (
        P(),
        P("sens", "pts", None),
        P(None, "pts", None),
        P("sens"),
        P("sens"),
        P(),
        P("pts"),
        P(None, "pts"),
        P(None, "pts"),
    )
    out_specs = P("sens", "pts", None)
    mapped = jax.shard_map(local, mesh=mesh, in_specs=in_specs, out_specs=out_specs, check_vma=False)

    def run(kernel, *rest):
        return mapped(jnp.asarray(dft_table(kernel.shape[-1])), kernel, *rest)

    return run
```

```python
import functools
import math

import jax
import jax.numpy as jnp
import ml_dtypes
import numpy as np
from jax import lax
from jax.experimental import pallas as pl
from jax.experimental.pallas import tpu as pltpu
from jax.sharding import PartitionSpec as P

COLS = 16
LANES = 128
SUB = 8
F32 = jnp.float32
BF16 = jnp.bfloat16
NT_DIMS = (((1,), (1,)), ((), ()))


def dft_table(length):
    steps = np.arange(length, dtype=np.int64)
    phase = (steps[:, None] * (2 * steps[None, :] + 1)) % (4 * length)
    angle = phase.astype(np.float64) * (2.0 * math.pi / (4 * length))
    pair = np.stack([np.cos(angle), -np.sin(angle)], axis=1)
    pair = pair.reshape(length, 2, length // LANES, LANES)
    table = pair.transpose(0, 2, 1, 3).reshape(length, 2 * length)
    high = table.astype(ml_dtypes.bfloat16)
    low = (table - high.astype(np.float64)).astype(ml_dtypes.bfloat16)
    return np.concatenate([high, low], axis=0)


def split(x):
    high = x.astype(BF16)
    return high, (x - high.astype(F32)).astype(BF16)


def dot(a, b):
    return jnp.dot(a, b, preferred_element_type=F32)


def dot_nt(a, b):
    return lax.dot_general(a, b, NT_DIMS, preferred_element_type=F32)


def inverse_dft(high, low, table_ref, length):
    return (
        dot_nt(high, table_ref[:length])
        + dot_nt(high, table_ref[length : 2 * length])
        + dot_nt(low, table_ref[:length])
    )


def in_vmem(x):
    return pltpu.with_memory_space_constraint(x, pltpu.VMEM)


def in_hbm(x):
    return pltpu.with_memory_space_constraint(x, pltpu.HBM)


def rows_at(start, size):
    return pl.ds(pl.multiple_of(start, size), size)


def forward_kernel(
    kern_hbm,
    vec_hbm,
    table_hbm,
    corr_hbm,
    pred_ref,
    khat_ref,
    table_ref,
    vec_ref,
    corr_ref,
    first_ref,
    second_ref,
    kern_ref,
    vhat_ref,
    lhs_ref,
    spec_ref,
    sems,
):
    sensors, points, length = kern_ref.shape
    count = vec_ref.shape[0]
    pitch = vhat_ref.shape[2] // count
    own, halo, _ = first_ref.shape
    shift = lax.axis_index("sens") * own
    odd_place = lax.axis_index("pts") % 2
    cols = length // LANES

    copies = [
        pltpu.make_async_copy(kern_hbm, kern_ref, sems.at[0]),
        pltpu.make_async_copy(table_hbm, table_ref.at[: 2 * length], sems.at[1]),
        pltpu.make_async_copy(table_hbm.at[:length], table_ref.at[2 * length :], sems.at[2]),
        pltpu.make_async_copy(vec_hbm, vec_ref, sems.at[3]),
        pltpu.make_async_copy(corr_hbm, corr_ref, sems.at[4]),
    ]
    for copy in copies:
        copy.start()

    def fill(source_ref, first):
        def step(i, _):
            rows = rows_at(i * points, points)
            high, low = split(source_ref[lax.rem(i + first, source_ref.shape[0])])
            lhs_ref[rows, :length] = high
            lhs_ref[rows, length : 2 * length] = high
            lhs_ref[rows, 2 * length :] = low
            return 0

        lax.fori_loop(0, source_ref.shape[0], step, 0)

    copies[0].wait()
    fill(kern_ref, 0)
    copies[1].wait()
    copies[2].wait()
    rows = sensors * points
    for col in range(cols):
        hat = dot(lhs_ref[:rows], table_ref[:, 2 * col * LANES : 2 * (col + 1) * LANES])
        real, imag = hat[:, :LANES], hat[:, LANES:]
        khat_ref[0, col] = real
        khat_ref[1, col] = imag - real
        khat_ref[2, col] = imag + real

    copies[3].wait()
    fill(vec_ref, shift)
    step_in = points - halo
    for k in range(own):
        at = lax.rem(k + shift, count)
        first_ref[k] = vec_ref[at, rows_at((1 - odd_place) * step_in, halo)]
        second_ref[k] = vec_ref[at, rows_at(odd_place * step_in, halo)]
    rows = count * points
    for col in range(cols):
        hat = dot(lhs_ref[:rows], table_ref[:, 2 * col * LANES : 2 * (col + 1) * LANES])
        for k in range(count):
            real = hat[k * points : (k + 1) * points, :LANES]
            imag = hat[k * points : (k + 1) * points, LANES:]
            vhat_ref[0, col, k * pitch : k * pitch + points] = real + imag
            vhat_ref[1, col, k * pitch : k * pitch + points] = real
            vhat_ref[2, col, k * pitch : k * pitch + points] = imag

    def product(col, _):
        acc = [[None] * 3 for _ in range(sensors)]
        for p in range(points):
            left = [vhat_ref[c, col, pl.ds(p, count, stride=pitch)] for c in range(3)]
            for s in range(sensors):
                for c in range(3):
                    row = khat_ref[c, col, s * points + p : s * points + p + 1]
                    term = left[c] * jnp.broadcast_to(row, left[c].shape)
                    acc[s][c] = term if acc[s][c] is None else acc[s][c] + term
        for s in range(sensors):
            one, two, three = acc[s]
            spec_ref[s * count : (s + 1) * count, rows_at(2 * col * LANES, LANES)] = one - three
            spec_ref[s * count : (s + 1) * count, rows_at((2 * col + 1) * LANES, LANES)] = one + two
        return 0

    lax.fori_loop(0, cols, product, 0)
    high, low = split(spec_ref[...])
    pred_ref[...] = inverse_dft(high, low, table_ref, length)
    copies[4].wait()


def forward(kernel, vectors, table, correlation, own):
    sensors, points, length = kernel.shape
    count = vectors.shape[0]
    cols = length // LANES
    most = max(sensors, count) * points
    hbm = pl.BlockSpec(memory_space=pltpu.HBM)
    return pl.pallas_call(
        forward_kernel,
        out_shape=(
            pltpu.VMEM((sensors * count, length), F32),
            pltpu.VMEM((3, cols, sensors * points, LANES), F32),
            pltpu.VMEM((3 * length, 2 * length), BF16),
            pltpu.VMEM(vectors.shape, F32),
            pltpu.VMEM(correlation.shape, F32),
            pltpu.VMEM((own, COLS, length), F32),
            pltpu.VMEM((own, COLS, length), F32),
        ),
        in_specs=[hbm] * 4,
        out_specs=[pl.BlockSpec(memory_space=pltpu.VMEM)] * 7,
        scratch_shapes=[
            pltpu.VMEM(kernel.shape, F32),
            pltpu.VMEM((3, cols, count * (points + SUB), LANES), F32),
            pltpu.VMEM((most, 3 * length), BF16),
            pltpu.VMEM((sensors * count, 2 * length), F32),
            pltpu.SemaphoreType.DMA((5,)),
        ],
        compiler_params=pltpu.CompilerParams(vmem_limit_bytes=12 * 1024 * 1024),
    )(*map(in_hbm, (kernel, vectors, table, correlation)))


def correlate(first, count, rhat_ref, khat_ref, table_ref, high_ref, low_ref):
    length = table_ref.shape[1] // 2
    sensors = rhat_ref.shape[2] // count
    points = khat_ref.shape[2] // sensors
    cols = length // LANES
    some = high_ref.shape[0] // points
    k_block, g_block = 4, 2
    tall = g_block * SUB
    blocks = points // tall

    def product(step, _):
        col, g0 = step // blocks, step % blocks
        for k0 in range(0, some, k_block):
            ks = range(k0, min(k0 + k_block, some))
            acc = {}
            for s in range(sensors):
                right = [
                    [
                        khat_ref[c, col, pl.ds(s * points + pl.multiple_of(g0 * tall, tall) + b * SUB, SUB)]
                        for c in range(3)
                    ]
                    for b in range(g_block)
                ]
                for k in ks:
                    for c in range(3):
                        at = s * count + first + k
                        left = jnp.broadcast_to(rhat_ref[c, col, at : at + 1], (SUB, LANES))
                        for b in range(g_block):
                            term = left * right[b][c]
                            acc[k, b, c] = term if s == 0 else acc[k, b, c] + term
            for k in ks:
                re = jnp.concatenate([acc[k, b, 0] + acc[k, b, 1] for b in range(g_block)], axis=0)
                im = jnp.concatenate([acc[k, b, 0] - acc[k, b, 2] for b in range(g_block)], axis=0)
                at = pl.ds(k * points + pl.multiple_of(g0 * tall, tall), tall)
                lanes = rows_at(2 * col * LANES, LANES)
                others = rows_at((2 * col + 1) * LANES, LANES)
                high_ref[at, lanes], low_ref[at, lanes] = split(re)
                high_ref[at, others], low_ref[at, others] = split(im)
        return 0

    lax.fori_loop(0, cols * blocks, product, 0)
    data = inverse_dft(high_ref[...], low_ref[...], table_ref, length)
    return data.reshape(some, points, length)


def others_kernel(
    own,
    count,
    scale_ref,
    group_ref,
    pred_ref,
    corr_ref,
    khat_ref,
    table_ref,
    rest_ref,
    rhat_ref,
    high_ref,
    low_ref,
):
    sensors = scale_ref.shape[0]
    rows, length = pred_ref.shape
    groups = corr_ref.shape[0] // length
    pred = pred_ref[...]
    high, low = split(pred)
    turned = jnp.concatenate([high.astype(F32), low.astype(F32)], axis=0).T
    lane = lax.broadcasted_iota(jnp.int32, turned.shape, 1)
    halves = jnp.concatenate([turned, jnp.where(lane < rows, turned, 0.0)], axis=0).astype(BF16)
    mixed = dot(corr_ref[...], halves)
    sensor = lax.rem(lane, rows) // count
    group = jnp.zeros_like(sensor)
    for s in range(sensors):
        group = jnp.where(sensor == s, group_ref[s], group)
    chosen = jnp.zeros_like(turned)
    for g in range(groups):
        chosen = jnp.where(group == g, mixed[g * length : (g + 1) * length], chosen)
    chosen = chosen.T
    whole = pred + chosen[:rows] + chosen[rows:]
    whole = jnp.concatenate(
        [whole[s * count : (s + 1) * count] * scale_ref[s] for s in range(sensors)], axis=0
    ) * (1.0 / (length * length))
    high, low = split(whole)
    hat = dot(jnp.concatenate([high, high, low], axis=1), table_ref[...])
    for col in range(length // LANES):
        real = hat[:, 2 * col * LANES : (2 * col + 1) * LANES]
        imag = hat[:, (2 * col + 1) * LANES : (2 * col + 2) * LANES]
        rhat_ref[0, col] = real + imag
        rhat_ref[1, col] = imag
        rhat_ref[2, col] = real
    rest_ref[...] = correlate(own, count, rhat_ref, khat_ref, table_ref, high_ref, low_ref)


def own_kernel(count, rhat_ref, khat_ref, table_ref, prior_ref, out_ref, high_ref, low_ref):
    data = correlate(0, count, rhat_ref, khat_ref, table_ref, high_ref, low_ref)
    out_ref[...] = data + prior_ref[...]


def adjoint_others(pred, scale, group, correlation, khat, table, own, count):
    rows, length = pred.shape
    points = khat.shape[2] // (rows // count)
    vmem = pl.BlockSpec(memory_space=pltpu.VMEM)
    smem = pl.BlockSpec(memory_space=pltpu.SMEM)
    some = count - own
    return pl.pallas_call(
        functools.partial(others_kernel, own, count),
        out_shape=(
            pltpu.VMEM((some, points, length), F32),
            pltpu.VMEM((3, length // LANES, rows, LANES), F32),
        ),
        in_specs=[smem] * 2 + [vmem] * 4,
        out_specs=[vmem, vmem],
        scratch_shapes=[pltpu.VMEM((some * points, 2 * length), BF16)] * 2,
        compiler_params=pltpu.CompilerParams(vmem_limit_bytes=12 * 1024 * 1024),
    )(scale, group, *map(in_vmem, (pred, correlation, khat, table)))


def adjoint_own(rhat, khat, table, prior, count):
    own, points, length = prior.shape
    vmem = pl.BlockSpec(memory_space=pltpu.VMEM)
    return pl.pallas_call(
        functools.partial(own_kernel, count),
        out_shape=pltpu.VMEM((own, points, length), F32),
        in_specs=[vmem] * 4,
        out_specs=vmem,
        scratch_shapes=[pltpu.VMEM((own * points, 2 * length), BF16)] * 2,
        compiler_params=pltpu.CompilerParams(vmem_limit_bytes=12 * 1024 * 1024),
        cost_estimate=pl.CostEstimate(
            flops=6 * own * points * length * length * 2, bytes_accessed=4 * khat.size, transcendentals=0
        ),
    )(*map(in_vmem, (rhat, khat, table, prior)))


def halves_kernel(corr_ref, out_ref):
    length = corr_ref.shape[1]

    def step(g, _):
        rows = rows_at(g * length, length)
        out_ref[rows, :length], out_ref[rows, length:] = split(corr_ref[g])
        return 0

    lax.fori_loop(0, corr_ref.shape[0], step, 0)


def halves_of(correlation):
    groups, length, _ = correlation.shape
    vmem = pl.BlockSpec(memory_space=pltpu.VMEM)
    return pl.pallas_call(
        halves_kernel,
        out_shape=pltpu.VMEM((groups * length, 2 * length), BF16),
        in_specs=[vmem],
        out_specs=vmem,
        compiler_params=pltpu.CompilerParams(vmem_limit_bytes=4 * 1024 * 1024),
    )(in_vmem(correlation))


def add_kernel(*refs):
    total = refs[0][...]
    for ref in refs[1:-1]:
        total = total + ref[...]
    refs[-1][...] = total


def add(*parts):
    vmem = pl.BlockSpec(memory_space=pltpu.VMEM)
    return pl.pallas_call(
        add_kernel,
        out_shape=jax.ShapeDtypeStruct(parts[0].shape, F32),
        in_specs=[vmem] * len(parts),
        out_specs=vmem,
        compiler_params=pltpu.CompilerParams(vmem_limit_bytes=4 * 1024 * 1024),
    )(*map(in_vmem, parts))


def prior_kernel(vec_ref, first_ref, second_ref, stiff_ref, coup_ref, near_ref, out_ref):
    own, points, _ = out_ref.shape
    place_here = lax.axis_index("pts")
    shift = lax.axis_index("sens") * own
    halo = first_ref.shape[1]
    count = vec_ref.shape[0]
    span = points + 2 * halo
    place = lax.broadcasted_iota(jnp.int32, (span, points), 0)
    coup = coup_ref[...]
    here = lax.broadcasted_iota(jnp.int32, (span, points), 1) + halo
    diagonal = stiff_ref[...] + jnp.sum(coup, axis=0, keepdims=True)
    weight = jnp.where(place == here, diagonal, 0.0)
    near = near_ref[...] - (place_here * points - halo)
    swap = (1 - place_here % 2) * (points + halo)
    near = near + jnp.where(near < halo, swap, 0) - jnp.where(near >= points + halo, swap, 0)
    for j in range(coup.shape[0]):
        weight = weight - jnp.where(place == near[j : j + 1], coup[j : j + 1], 0.0)
    weight_high, weight_low = split(weight.T)
    for k in range(own):
        value = jnp.concatenate(
            [first_ref[k], vec_ref[lax.rem(shift + k, count)], second_ref[k]], axis=0
        )
        high, low = split(value)
        out_ref[k] = dot(weight_high, high) + dot(weight_high, low) + dot(weight_low, high)


def prior_term(vectors, first, second, stiffness, couplings, neighbors):
    own = first.shape[0]
    _, points, length = vectors.shape
    vmem = pl.BlockSpec(memory_space=pltpu.VMEM)
    return pl.pallas_call(
        prior_kernel,
        out_shape=pltpu.VMEM((own, points, length), F32),
        in_specs=[vmem] * 6,
        out_specs=vmem,
        compiler_params=pltpu.CompilerParams(vmem_limit_bytes=8 * 1024 * 1024),
    )(
        *map(in_vmem, (vectors, first, second, stiffness[None], couplings, neighbors))
    )


def stages(size):
    bits = [1 << bit for bit in range(size.bit_length() - 1)]
    masks = []
    while bits:
        low, *bits = bits
        masks.append([low])
        if bits:
            high, *bits = bits
            masks[-1] += [high, low + high]
    turned = list(masks)
    if len(masks) > 1 and len(masks[0]) == len(masks[1]):
        turned[0], turned[1] = masks[1], masks[0]
    return masks, turned


def local(table, kernel, vectors, noise_scale, sensor_group, correlation, stiffness, couplings, neighbors):
    sensors, points, length = kernel.shape
    count = vectors.shape[0]
    n_sens, n_pts = lax.axis_size("sens"), lax.axis_size("pts")
    own = count // n_sens

    pred, khat, table, vectors, correlation, *edges = forward(
        kernel, vectors, table, correlation, own
    )
    correlation = halves_of(correlation)

    links = [[], []]
    for p in range(n_pts - 1):
        links[p % 2] += [(p, p + 1), (p + 1, p)]
    halos = []
    for step, (even, odd) in enumerate(zip(*stages(n_pts))):
        if step == 1:
            pred, edges[1] = lax.optimization_barrier((pred, edges[1]))
        more = []
        for mask_even, mask_odd in zip(even, odd):
            pairs = [
                (s * n_pts + p, s * n_pts + (p ^ (mask_odd if s % 2 else mask_even)))
                for s in range(n_sens)
                for p in range(n_pts)
            ]
            more.append(lax.ppermute(pred, ("sens", "pts"), pairs))
        if step < 2:
            halos.append(lax.ppermute(edges[step], "pts", links[step]))
        for part in more:
            pred = pred + part
        if step == 0:
            pred, halos[0], correlation = lax.optimization_barrier((pred, halos[0], correlation))

    prior = prior_term(vectors, halos[0], halos[1], stiffness, couplings, neighbors)
    pred, prior = lax.optimization_barrier((pred, prior))
    rest, rhat = adjoint_others(pred, noise_scale, sensor_group, correlation, khat, table, own, count)
    received = []
    for j in range(1, n_sens):
        pairs = [(s, (s + j) % n_sens) for s in range(n_sens)]
        received.append(lax.ppermute(rest[(j - 1) * own : j * own], "sens", pairs))
    total = adjoint_own(rhat, khat, table, prior, count)
    return add(total, *received)


def solution(mesh):
    in_specs = (
        P(),
        P("sens", "pts", None),
        P(None, "pts", None),
        P("sens"),
        P("sens"),
        P(),
        P("pts"),
        P(None, "pts"),
        P(None, "pts"),
    )
    out_specs = P("sens", "pts", None)
    mapped = jax.shard_map(local, mesh=mesh, in_specs=in_specs, out_specs=out_specs, check_vma=False)

    def run(kernel, *rest):
        return mapped(jnp.asarray(dft_table(kernel.shape[-1])), kernel, *rest)

    return run
```

```python
import functools
import math

import jax
import jax.numpy as jnp
import ml_dtypes
import numpy as np
from jax import lax
from jax.experimental import pallas as pl
from jax.experimental.pallas import tpu as pltpu
from jax.sharding import PartitionSpec as P

COLS = 16
LANES = 128
SUB = 8
F32 = jnp.float32
BF16 = jnp.bfloat16


def halves_table(table):
    high = table.astype(ml_dtypes.bfloat16)
    low = (table - high.astype(np.float64)).astype(ml_dtypes.bfloat16)
    return np.concatenate([high, low], axis=0)


def dft_tables(length):
    steps = np.arange(length, dtype=np.int64)
    phase = (steps[:, None] * (2 * steps[None, :] + 1)) % (4 * length)
    angle = phase.astype(np.float64) * (2.0 * math.pi / (4 * length))
    pair = np.stack([np.cos(angle), -np.sin(angle)], axis=1)
    pair = pair.reshape(length, 2, length // LANES, LANES)
    table = pair.transpose(0, 2, 1, 3).reshape(length, 2 * length)
    return halves_table(table), halves_table(table.T)


def split(x):
    high = x.astype(BF16)
    return high, (x - high.astype(F32)).astype(BF16)


def dot(a, b):
    return jnp.dot(a, b, preferred_element_type=F32)


def in_vmem(x):
    return pltpu.with_memory_space_constraint(x, pltpu.VMEM)


def in_hbm(x):
    return pltpu.with_memory_space_constraint(x, pltpu.HBM)


def rows_at(start, size):
    return pl.ds(pl.multiple_of(start, size), size)


def back_column(high, low, inverse_ref, col):
    half = inverse_ref.shape[0] // 2
    upper = inverse_ref[2 * col * LANES : 2 * (col + 1) * LANES]
    lower = inverse_ref[half + 2 * col * LANES : half + 2 * (col + 1) * LANES]
    return dot(high, upper) + dot(high, lower) + dot(low, upper)


def forward_kernel(
    kern_hbm,
    vec_hbm,
    table_hbm,
    inverse_hbm,
    corr_hbm,
    pred_ref,
    khat_ref,
    table_ref,
    inverse_ref,
    vec_ref,
    corr_ref,
    first_ref,
    second_ref,
    kern_ref,
    vhat_ref,
    kern_lhs_ref,
    vec_lhs_ref,
    sems,
):
    sensors, points, length = kern_ref.shape
    count = vec_ref.shape[0]
    own, halo, _ = first_ref.shape
    shift = lax.axis_index("sens") * own
    odd_place = lax.axis_index("pts") % 2
    cols = length // LANES

    pairs = [(kern_hbm, kern_ref), (vec_hbm, vec_ref)]
    for col in range(cols):
        lanes = slice(2 * col * LANES, 2 * (col + 1) * LANES)
        pairs.append((table_hbm.at[:, lanes], table_ref.at[: 2 * length, lanes]))
        pairs.append((table_hbm.at[:length, lanes], table_ref.at[2 * length :, lanes]))
    pairs.append((inverse_hbm, inverse_ref))
    pairs.append((corr_hbm, corr_ref))
    copies = [
        pltpu.make_async_copy(source, target, sems.at[i]) for i, (source, target) in enumerate(pairs)
    ]
    for i in (0, 2, 3, 1, *range(4, len(copies))):
        copies[i].start()

    def fill(source_ref, lhs_ref, first):
        def step(i, _):
            rows = rows_at(i * points, points)
            high, low = split(source_ref[lax.rem(i + first, source_ref.shape[0])])
            lhs_ref[rows, :length] = high
            lhs_ref[rows, length : 2 * length] = high
            lhs_ref[rows, 2 * length :] = low
            return 0

        lax.fori_loop(0, source_ref.shape[0], step, 0)

    def transform(lhs_ref, col):
        hat = dot(lhs_ref[...], table_ref[:, 2 * col * LANES : 2 * (col + 1) * LANES])
        return hat[:, :LANES], hat[:, LANES:]

    def kern_column(col):
        real, imag = transform(kern_lhs_ref, col)
        khat_ref[0, col] = real
        khat_ref[1, col] = imag - real
        khat_ref[2, col] = imag + real

    def vec_column(col):
        real, imag = transform(vec_lhs_ref, col)
        for k in range(count):
            re, im = real[k * points : (k + 1) * points], imag[k * points : (k + 1) * points]
            at = pl.ds(k, points, stride=count)
            vhat_ref[0, col, at] = re + im
            vhat_ref[1, col, at] = re
            vhat_ref[2, col, at] = im

    def product(col):
        acc = [[None] * 3 for _ in range(sensors)]
        for p in range(points):
            left = [vhat_ref[c, col, p * count : (p + 1) * count] for c in range(3)]
            for s in range(sensors):
                for c in range(3):
                    row = khat_ref[c, col, s * points + p : s * points + p + 1]
                    term = left[c] * jnp.broadcast_to(row, left[c].shape)
                    acc[s][c] = term if acc[s][c] is None else acc[s][c] + term
        real = jnp.concatenate([one - three for one, _, three in acc], axis=0)
        imag = jnp.concatenate([one + two for one, two, _ in acc], axis=0)
        high, low = split(jnp.concatenate([real, imag], axis=1))
        return back_column(high, low, inverse_ref, col)

    copies[0].wait()
    fill(kern_ref, kern_lhs_ref, 0)
    copies[2].wait()
    copies[3].wait()
    kern_column(0)
    copies[1].wait()
    fill(vec_ref, vec_lhs_ref, shift)
    step_in = points - halo
    for k in range(own):
        at = lax.rem(k + shift, count)
        first_ref[k] = vec_ref[at, rows_at((1 - odd_place) * step_in, halo)]
        second_ref[k] = vec_ref[at, rows_at(odd_place * step_in, halo)]
    for copy in copies[4:-1]:
        copy.wait()
    pred = None
    for col in range(cols):
        if col:
            kern_column(col)
        vec_column(col)
        part = product(col)
        pred = part if pred is None else pred + part
    pred_ref[...] = pred
    copies[-1].wait()


def forward(kernel, vectors, table, inverse, correlation, own):
    sensors, points, length = kernel.shape
    count = vectors.shape[0]
    cols = length // LANES
    hbm = pl.BlockSpec(memory_space=pltpu.HBM)
    return pl.pallas_call(
        forward_kernel,
        out_shape=(
            pltpu.VMEM((sensors * count, length), F32),
            pltpu.VMEM((3, cols, sensors * points, LANES), F32),
            pltpu.VMEM((3 * length, 2 * length), BF16),
            pltpu.VMEM((4 * length, length), BF16),
            pltpu.VMEM(vectors.shape, F32),
            pltpu.VMEM(correlation.shape, F32),
            pltpu.VMEM((own, COLS, length), F32),
            pltpu.VMEM((own, COLS, length), F32),
        ),
        in_specs=[hbm] * 5,
        out_specs=[pl.BlockSpec(memory_space=pltpu.VMEM)] * 8,
        scratch_shapes=[
            pltpu.VMEM(kernel.shape, F32),
            pltpu.VMEM((3, cols, count * points, LANES), F32),
            pltpu.VMEM((sensors * points, 3 * length), BF16),
            pltpu.VMEM((count * points, 3 * length), BF16),
            pltpu.SemaphoreType.DMA((4 + 2 * cols,)),
        ],
        compiler_params=pltpu.CompilerParams(vmem_limit_bytes=14 * 1024 * 1024),
    )(*map(in_hbm, (kernel, vectors, table, inverse, correlation)))


def correlate(first, count, rhat_ref, khat_ref, inverse_ref, high_ref, low_ref):
    length = inverse_ref.shape[1]
    sensors = rhat_ref.shape[2] // count
    points = khat_ref.shape[2] // sensors
    cols = length // LANES
    some = high_ref.shape[0] // points
    k_block, g_block = 4, 2
    tall = g_block * SUB
    blocks = points // tall

    def product(step, _):
        col, g0 = step // blocks, step % blocks
        for k0 in range(0, some, k_block):
            ks = range(k0, min(k0 + k_block, some))
            acc = {}
            for s in range(sensors):
                right = [
                    [
                        khat_ref[c, col, pl.ds(s * points + pl.multiple_of(g0 * tall, tall) + b * SUB, SUB)]
                        for c in range(3)
                    ]
                    for b in range(g_block)
                ]
                for k in ks:
                    for c in range(3):
                        at = s * count + first + k
                        left = jnp.broadcast_to(rhat_ref[c, col, at : at + 1], (SUB, LANES))
                        for b in range(g_block):
                            term = left * right[b][c]
                            acc[k, b, c] = term if s == 0 else acc[k, b, c] + term
            for k in ks:
                re = jnp.concatenate([acc[k, b, 0] + acc[k, b, 1] for b in range(g_block)], axis=0)
                im = jnp.concatenate([acc[k, b, 0] - acc[k, b, 2] for b in range(g_block)], axis=0)
                at = pl.ds(k * points + pl.multiple_of(g0 * tall, tall), tall)
                lanes = rows_at(2 * col * LANES, LANES)
                others = rows_at((2 * col + 1) * LANES, LANES)
                high_ref[at, lanes], low_ref[at, lanes] = split(re)
                high_ref[at, others], low_ref[at, others] = split(im)
        return 0

    lax.fori_loop(0, cols * blocks, product, 0)
    high, low = high_ref[...], low_ref[...]
    upper, lower = inverse_ref[: 2 * length], inverse_ref[2 * length :]
    data = dot(high, upper) + dot(high, lower) + dot(low, upper)
    return data.reshape(some, points, length)


def others_kernel(
    own,
    count,
    scale_ref,
    group_ref,
    pred_ref,
    corr_ref,
    khat_ref,
    table_ref,
    inverse_ref,
    rest_ref,
    rhat_ref,
    high_ref,
    low_ref,
):
    sensors = scale_ref.shape[0]
    length = pred_ref.shape[1]
    groups = corr_ref.shape[1] // length
    pred = pred_ref[...]
    high, low = split(pred)
    mixed = dot(jnp.concatenate([high, high], axis=1), corr_ref[...]) + dot(low, corr_ref[:length])
    whole = []
    for s in range(sensors):
        at = slice(s * count, (s + 1) * count)
        value = pred[at]
        for g in range(groups):
            weight = jnp.where(group_ref[s] == g, 1.0, 0.0)
            value = value + weight * mixed[at, g * length : (g + 1) * length]
        whole.append(value * (scale_ref[s] * (1.0 / (length * length))))
    high, low = split(jnp.concatenate(whole, axis=0))
    hat = dot(jnp.concatenate([high, high, low], axis=1), table_ref[...])
    for col in range(length // LANES):
        real = hat[:, 2 * col * LANES : (2 * col + 1) * LANES]
        imag = hat[:, (2 * col + 1) * LANES : (2 * col + 2) * LANES]
        rhat_ref[0, col] = real + imag
        rhat_ref[1, col] = imag
        rhat_ref[2, col] = real
    rest_ref[...] = correlate(own, count, rhat_ref, khat_ref, inverse_ref, high_ref, low_ref)


def own_kernel(count, rhat_ref, khat_ref, inverse_ref, prior_ref, out_ref, high_ref, low_ref):
    data = correlate(0, count, rhat_ref, khat_ref, inverse_ref, high_ref, low_ref)
    out_ref[...] = data + prior_ref[...]


def adjoint_others(pred, scale, group, correlation, khat, table, inverse, own, count):
    rows, length = pred.shape
    points = khat.shape[2] // (rows // count)
    vmem = pl.BlockSpec(memory_space=pltpu.VMEM)
    smem = pl.BlockSpec(memory_space=pltpu.SMEM)
    some = count - own
    return pl.pallas_call(
        functools.partial(others_kernel, own, count),
        out_shape=(
            pltpu.VMEM((some, points, length), F32),
            pltpu.VMEM((3, length // LANES, rows, LANES), F32),
        ),
        in_specs=[smem] * 2 + [vmem] * 5,
        out_specs=[vmem, vmem],
        scratch_shapes=[pltpu.VMEM((some * points, 2 * length), BF16)] * 2,
        compiler_params=pltpu.CompilerParams(vmem_limit_bytes=12 * 1024 * 1024),
        cost_estimate=pl.CostEstimate(flops=1, bytes_accessed=1, transcendentals=0),
    )(scale, group, *map(in_vmem, (pred, correlation, khat, table, inverse)))


def adjoint_own(rhat, khat, inverse, prior, count):
    own, points, length = prior.shape
    vmem = pl.BlockSpec(memory_space=pltpu.VMEM)
    return pl.pallas_call(
        functools.partial(own_kernel, count),
        out_shape=pltpu.VMEM((own, points, length), F32),
        in_specs=[vmem] * 4,
        out_specs=vmem,
        scratch_shapes=[pltpu.VMEM((own * points, 2 * length), BF16)] * 2,
        compiler_params=pltpu.CompilerParams(vmem_limit_bytes=12 * 1024 * 1024),
        cost_estimate=pl.CostEstimate(
            flops=6 * own * points * length * length * 2, bytes_accessed=4 * khat.size, transcendentals=0
        ),
    )(*map(in_vmem, (rhat, khat, inverse, prior)))


def turned_kernel(corr_ref, out_ref):
    groups, length, _ = corr_ref.shape
    for g in range(groups):
        lanes = slice(g * length, (g + 1) * length)
        out_ref[:length, lanes], out_ref[length:, lanes] = split(corr_ref[g].T)


def turned(correlation):
    groups, length, _ = correlation.shape
    vmem = pl.BlockSpec(memory_space=pltpu.VMEM)
    return pl.pallas_call(
        turned_kernel,
        out_shape=pltpu.VMEM((2 * length, groups * length), BF16),
        in_specs=[vmem],
        out_specs=vmem,
        compiler_params=pltpu.CompilerParams(vmem_limit_bytes=8 * 1024 * 1024),
    )(in_vmem(correlation))


def add_kernel(*refs):
    total = refs[0][...]
    for ref in refs[1:-1]:
        total = total + ref[...]
    refs[-1][...] = total


def add(*parts):
    vmem = pl.BlockSpec(memory_space=pltpu.VMEM)
    return pl.pallas_call(
        add_kernel,
        out_shape=jax.ShapeDtypeStruct(parts[0].shape, F32),
        in_specs=[vmem] * len(parts),
        out_specs=vmem,
        compiler_params=pltpu.CompilerParams(vmem_limit_bytes=4 * 1024 * 1024),
    )(*map(in_vmem, parts))


def prior_kernel(vec_ref, first_ref, second_ref, stiff_ref, coup_ref, near_ref, out_ref):
    own, points, _ = out_ref.shape
    place_here = lax.axis_index("pts")
    shift = lax.axis_index("sens") * own
    halo = first_ref.shape[1]
    count = vec_ref.shape[0]
    span = points + 2 * halo
    place = lax.broadcasted_iota(jnp.int32, (span, points), 0)
    coup = coup_ref[...]
    here = lax.broadcasted_iota(jnp.int32, (span, points), 1) + halo
    diagonal = stiff_ref[...] + jnp.sum(coup, axis=0, keepdims=True)
    weight = jnp.where(place == here, diagonal, 0.0)
    near = near_ref[...] - (place_here * points - halo)
    swap = (1 - place_here % 2) * (points + halo)
    near = near + jnp.where(near < halo, swap, 0) - jnp.where(near >= points + halo, swap, 0)
    for j in range(coup.shape[0]):
        weight = weight - jnp.where(place == near[j : j + 1], coup[j : j + 1], 0.0)
    weight_high, weight_low = split(weight.T)
    for k in range(own):
        value = jnp.concatenate(
            [first_ref[k], vec_ref[lax.rem(shift + k, count)], second_ref[k]], axis=0
        )
        high, low = split(value)
        out_ref[k] = dot(weight_high, high) + dot(weight_high, low) + dot(weight_low, high)


def prior_term(vectors, first, second, stiffness, couplings, neighbors):
    own = first.shape[0]
    _, points, length = vectors.shape
    vmem = pl.BlockSpec(memory_space=pltpu.VMEM)
    return pl.pallas_call(
        prior_kernel,
        out_shape=pltpu.VMEM((own, points, length), F32),
        in_specs=[vmem] * 6,
        out_specs=vmem,
        compiler_params=pltpu.CompilerParams(vmem_limit_bytes=8 * 1024 * 1024),
    )(
        *map(in_vmem, (vectors, first, second, stiffness[None], couplings, neighbors))
    )


def stages(size):
    bits = [1 << bit for bit in range(size.bit_length() - 1)]
    masks = []
    while bits:
        low, *bits = bits
        masks.append([low])
        if bits:
            high, *bits = bits
            masks[-1] += [high, low + high]
    turned = list(masks)
    if len(masks) > 1 and len(masks[0]) == len(masks[1]):
        turned[0], turned[1] = masks[1], masks[0]
    return masks, turned


def local(table, inverse, kernel, vectors, noise_scale, sensor_group, correlation, stiffness, couplings, neighbors):
    sensors, points, length = kernel.shape
    count = vectors.shape[0]
    n_sens, n_pts = lax.axis_size("sens"), lax.axis_size("pts")
    own = count // n_sens

    pred, khat, table, inverse, vectors, correlation, *edges = forward(
        kernel, vectors, table, inverse, correlation, own
    )
    correlation = turned(correlation)

    links = [[], []]
    for s in range(n_sens):
        for p in range(n_pts - 1):
            here = s * n_pts + p
            links[p % 2] += [(here, here + 1), (here + 1, here)]
        if n_sens % 2 == 0:
            for p in (0, n_pts - 1):
                links[1].append((s * n_pts + p, (s ^ 1) * n_pts + p))
    halos = []
    for step, (even, odd) in enumerate(zip(*stages(n_pts))):
        if step == 1:
            pred, edges[1] = lax.optimization_barrier((pred, edges[1]))
        more = []
        for mask_even, mask_odd in zip(even, odd):
            pairs = [
                (s * n_pts + p, s * n_pts + (p ^ (mask_odd if s % 2 else mask_even)))
                for s in range(n_sens)
                for p in range(n_pts)
            ]
            more.append(lax.ppermute(pred, ("sens", "pts"), pairs))
        if step < 2:
            halos.append(lax.ppermute(edges[step], ("sens", "pts"), links[step]))
        for part in more:
            pred = pred + part
        if step == 0:
            pred, halos[0], correlation = lax.optimization_barrier((pred, halos[0], correlation))

    rest, rhat = adjoint_others(pred, noise_scale, sensor_group, correlation, khat, table, inverse, own, count)
    rest, halos[1] = lax.optimization_barrier((rest, halos[1]))
    received = []
    for j in range(1, n_sens):
        pairs = [(s, (s + j) % n_sens) for s in range(n_sens)]
        received.append(lax.ppermute(rest[(j - 1) * own : j * own], "sens", pairs))
    prior = prior_term(vectors, halos[0], halos[1], stiffness, couplings, neighbors)
    total = adjoint_own(rhat, khat, inverse, prior, count)
    return add(total, *received)


def solution(mesh):
    in_specs = (
        P(),
        P(),
        P("sens", "pts", None),
        P(None, "pts", None),
        P("sens"),
        P("sens"),
        P(),
        P("pts"),
        P(None, "pts"),
        P(None, "pts"),
    )
    out_specs = P("sens", "pts", None)
    mapped = jax.shard_map(local, mesh=mesh, in_specs=in_specs, out_specs=out_specs, check_vma=False)

    def run(kernel, *rest):
        tables = map(jnp.asarray, dft_tables(kernel.shape[-1]))
        return mapped(*tables, kernel, *rest)

    return run
```

```python
import functools
import math

import jax
import jax.numpy as jnp
import ml_dtypes
import numpy as np
from jax import lax
from jax.experimental import pallas as pl
from jax.experimental.pallas import tpu as pltpu
from jax.sharding import PartitionSpec as P

COLS = 16
LANES = 128
SUB = 8
F32 = jnp.float32
BF16 = jnp.bfloat16


def halves_table(table):
    high = table.astype(ml_dtypes.bfloat16)
    low = (table - high.astype(np.float64)).astype(ml_dtypes.bfloat16)
    return np.concatenate([high, low], axis=0)


def dft_tables(length):
    steps = np.arange(length, dtype=np.int64)
    phase = (steps[:, None] * (2 * steps[None, :] + 1)) % (4 * length)
    angle = phase.astype(np.float64) * (2.0 * math.pi / (4 * length))
    pair = np.stack([np.cos(angle), -np.sin(angle)], axis=1)
    pair = pair.reshape(length, 2, length // LANES, LANES)
    table = pair.transpose(0, 2, 1, 3).reshape(length, 2 * length)
    return halves_table(table), halves_table(table.T)


def split(x):
    high = x.astype(BF16)
    return high, (x - high.astype(F32)).astype(BF16)


def dot(a, b):
    return jnp.dot(a, b, preferred_element_type=F32)


def in_vmem(x):
    return pltpu.with_memory_space_constraint(x, pltpu.VMEM)


def in_hbm(x):
    return pltpu.with_memory_space_constraint(x, pltpu.HBM)


def rows_at(start, size):
    return pl.ds(pl.multiple_of(start, size), size)


def sums(parts):
    row = lax.broadcasted_iota(jnp.int32, parts[0].shape, 0)
    width = 1
    while len(parts) > 1:
        first = row // width % 2 == 0
        parts = [
            jnp.where(first, a, b) + pltpu.roll(jnp.where(first, b, a), width, 0)
            for a, b in zip(parts[::2], parts[1::2])
        ]
        width *= 2
    return parts[0]


def back(high_ref, low_ref, inverse_ref):
    half = inverse_ref.shape[0] // 2
    high, low = high_ref[...], low_ref[...]
    upper, lower = inverse_ref[:half], inverse_ref[half:]
    return dot(high, upper) + dot(high, lower) + dot(low, upper)


def forward_kernel(
    kern_hbm,
    vec_hbm,
    table_hbm,
    inverse_hbm,
    corr_hbm,
    pred_ref,
    khat_ref,
    table_ref,
    inverse_ref,
    vec_ref,
    corr_ref,
    first_ref,
    second_ref,
    kern_ref,
    vhat_ref,
    kern_lhs_ref,
    vec_lhs_ref,
    high_ref,
    low_ref,
    sems,
):
    sensors, points, length = kern_ref.shape
    count = vec_ref.shape[0]
    own, halo, _ = first_ref.shape
    shift = lax.axis_index("sens") * own
    odd_place = lax.axis_index("pts") % 2
    cols = length // LANES

    pairs = [(kern_hbm, kern_ref), (vec_hbm, vec_ref)]
    for col in range(cols):
        lanes = slice(2 * col * LANES, 2 * (col + 1) * LANES)
        pairs.append((table_hbm.at[:, lanes], table_ref.at[: 2 * length, lanes]))
        pairs.append((table_hbm.at[:length, lanes], table_ref.at[2 * length :, lanes]))
    pairs.append((inverse_hbm, inverse_ref))
    pairs.append((corr_hbm, corr_ref))
    copies = [
        pltpu.make_async_copy(source, target, sems.at[i]) for i, (source, target) in enumerate(pairs)
    ]
    for i in (0, 2, 3, 1, *range(4, len(copies))):
        copies[i].start()

    def fill(source_ref, lhs_ref, first):
        def step(i, _):
            rows = rows_at(i * points, points)
            high, low = split(source_ref[lax.rem(i + first, source_ref.shape[0])])
            lhs_ref[rows, :length] = high
            lhs_ref[rows, length : 2 * length] = high
            lhs_ref[rows, 2 * length :] = low
            return 0

        lax.fori_loop(0, source_ref.shape[0], step, 0)

    def transform(lhs_ref, col):
        hat = dot(lhs_ref[...], table_ref[:, 2 * col * LANES : 2 * (col + 1) * LANES])
        return hat[:, :LANES], hat[:, LANES:]

    def kern_column(col):
        real, imag = transform(kern_lhs_ref, col)
        khat_ref[0, col] = real
        khat_ref[1, col] = imag - real
        khat_ref[2, col] = imag + real

    def vec_column(col):
        real, imag = transform(vec_lhs_ref, col)
        vhat_ref[0, col] = real + imag
        vhat_ref[1, col] = real
        vhat_ref[2, col] = imag

    def product(col):
        rows = []
        for s in range(sensors):
            acc = [[None] * 3 for _ in range(count)]
            for g in range(points // SUB):
                at = s * points + g * SUB
                right = [khat_ref[c, col, at : at + SUB] for c in range(3)]
                for k in range(count):
                    for c in range(3):
                        at = k * points + g * SUB
                        term = vhat_ref[c, col, at : at + SUB] * right[c]
                        acc[k][c] = term if acc[k][c] is None else acc[k][c] + term
            real = sums([one - three for one, _, three in acc])
            imag = sums([one + two for one, two, _ in acc])
            rows.append(jnp.concatenate([real, imag], axis=1))
        lanes = slice(2 * col * LANES, 2 * (col + 1) * LANES)
        high_ref[:, lanes], low_ref[:, lanes] = split(jnp.concatenate(rows, axis=0))

    copies[0].wait()
    fill(kern_ref, kern_lhs_ref, 0)
    copies[2].wait()
    copies[3].wait()
    kern_column(0)
    copies[1].wait()
    fill(vec_ref, vec_lhs_ref, shift)
    step_in = points - halo
    for k in range(own):
        at = lax.rem(k + shift, count)
        first_ref[k] = vec_ref[at, rows_at((1 - odd_place) * step_in, halo)]
        second_ref[k] = vec_ref[at, rows_at(odd_place * step_in, halo)]
    for copy in copies[4:-1]:
        copy.wait()
    vec_column(0)
    for col in range(cols):
        if col + 1 < cols:
            kern_column(col + 1)
            vec_column(col + 1)
        product(col)
    pred_ref[...] = back(high_ref, low_ref, inverse_ref)
    copies[-1].wait()


def forward(kernel, vectors, table, inverse, correlation, own):
    sensors, points, length = kernel.shape
    count = vectors.shape[0]
    cols = length // LANES
    hbm = pl.BlockSpec(memory_space=pltpu.HBM)
    return pl.pallas_call(
        forward_kernel,
        out_shape=(
            pltpu.VMEM((sensors * count, length), F32),
            pltpu.VMEM((3, cols, sensors * points, LANES), F32),
            pltpu.VMEM((3 * length, 2 * length), BF16),
            pltpu.VMEM((4 * length, length), BF16),
            pltpu.VMEM(vectors.shape, F32),
            pltpu.VMEM(correlation.shape, F32),
            pltpu.VMEM((own, COLS, length), F32),
            pltpu.VMEM((own, COLS, length), F32),
        ),
        in_specs=[hbm] * 5,
        out_specs=[pl.BlockSpec(memory_space=pltpu.VMEM)] * 8,
        scratch_shapes=[
            pltpu.VMEM(kernel.shape, F32),
            pltpu.VMEM((3, cols, count * points, LANES), F32),
            pltpu.VMEM((sensors * points, 3 * length), BF16),
            pltpu.VMEM((count * points, 3 * length), BF16),
            pltpu.VMEM((sensors * count, 2 * length), BF16),
            pltpu.VMEM((sensors * count, 2 * length), BF16),
            pltpu.SemaphoreType.DMA((4 + 2 * cols,)),
        ],
        compiler_params=pltpu.CompilerParams(vmem_limit_bytes=14 * 1024 * 1024),
    )(*map(in_hbm, (kernel, vectors, table, inverse, correlation)))


def correlate(first, count, rhat_ref, khat_ref, inverse_ref, high_ref, low_ref, data_ref):
    some, points, length = data_ref.shape
    sensors = rhat_ref.shape[2] // count
    cols = length // LANES
    k_block, g_block = 4, 2
    tall = g_block * SUB

    def product(col, g0, ks):
        acc = {}
        for s in range(sensors):
            right = [
                [
                    khat_ref[c, col, pl.ds(s * points + g0 * tall + b * SUB, SUB)]
                    for c in range(3)
                ]
                for b in range(g_block)
            ]
            for k in ks:
                for c in range(3):
                    at = s * count + first + k
                    left = jnp.broadcast_to(rhat_ref[c, col, at : at + 1], (SUB, LANES))
                    for b in range(g_block):
                        term = left * right[b][c]
                        acc[k, b, c] = term if s == 0 else acc[k, b, c] + term
        for k in ks:
            re = jnp.concatenate([acc[k, b, 0] + acc[k, b, 1] for b in range(g_block)], axis=0)
            im = jnp.concatenate([acc[k, b, 0] - acc[k, b, 2] for b in range(g_block)], axis=0)
            at = slice(k * points + g0 * tall, k * points + (g0 + 1) * tall)
            lanes = slice(2 * col * LANES, (2 * col + 1) * LANES)
            others = slice((2 * col + 1) * LANES, (2 * col + 2) * LANES)
            high_ref[at, lanes], low_ref[at, lanes] = split(re)
            high_ref[at, others], low_ref[at, others] = split(im)

    for col in range(cols):
        for g0 in range(points // tall):
            for k0 in range(0, some, k_block):
                product(col, g0, range(k0, min(k0 + k_block, some)))
        lanes = slice(2 * col * LANES, 2 * (col + 1) * LANES)
        upper = inverse_ref[lanes]
        lower = inverse_ref[lanes.start + 2 * length : lanes.stop + 2 * length]
        high, low = high_ref[:, lanes], low_ref[:, lanes]
        part = dot(high, upper) + dot(high, lower) + dot(low, upper)
        part = part.reshape(some, points, length)
        data_ref[...] = data_ref[...] + part if col else part


def others_kernel(
    own,
    count,
    scale_ref,
    group_ref,
    pred_ref,
    corr_ref,
    khat_ref,
    table_ref,
    inverse_ref,
    rest_ref,
    rhat_ref,
    high_ref,
    low_ref,
):
    sensors = scale_ref.shape[0]
    length = pred_ref.shape[1]
    groups = corr_ref.shape[1] // length
    pred = pred_ref[...]
    high, low = split(pred)
    mixed = dot(jnp.concatenate([high, high], axis=1), corr_ref[...]) + dot(low, corr_ref[:length])
    whole = []
    for s in range(sensors):
        at = slice(s * count, (s + 1) * count)
        value = pred[at]
        for g in range(groups):
            weight = jnp.where(group_ref[s] == g, 1.0, 0.0)
            value = value + weight * mixed[at, g * length : (g + 1) * length]
        whole.append(value * (scale_ref[s] * (1.0 / (length * length))))
    high, low = split(jnp.concatenate(whole, axis=0))
    hat = dot(jnp.concatenate([high, high, low], axis=1), table_ref[...])
    for col in range(length // LANES):
        real = hat[:, 2 * col * LANES : (2 * col + 1) * LANES]
        imag = hat[:, (2 * col + 1) * LANES : (2 * col + 2) * LANES]
        rhat_ref[0, col] = real + imag
        rhat_ref[1, col] = imag
        rhat_ref[2, col] = real
    correlate(own, count, rhat_ref, khat_ref, inverse_ref, high_ref, low_ref, rest_ref)


def own_kernel(
    count,
    rhat_ref,
    khat_ref,
    inverse_ref,
    vec_ref,
    weight_ref,
    first_ref,
    second_ref,
    out_ref,
    high_ref,
    low_ref,
):
    correlate(0, count, rhat_ref, khat_ref, inverse_ref, high_ref, low_ref, out_ref)
    own = out_ref.shape[0]
    sens = lax.axis_index("sens")
    upper, lower = weight_ref[0], weight_ref[1]
    for k in range(own):
        here = vec_ref[lax.rem(sens * own + k, count)]
        value = jnp.concatenate([first_ref[k], here, second_ref[k]], axis=0)
        high, low = split(value)
        out_ref[k] = out_ref[k] + dot(upper, high) + dot(upper, low) + dot(lower, high)


def adjoint_others(pred, scale, group, correlation, khat, table, inverse, own, count):
    rows, length = pred.shape
    points = khat.shape[2] // (rows // count)
    vmem = pl.BlockSpec(memory_space=pltpu.VMEM)
    smem = pl.BlockSpec(memory_space=pltpu.SMEM)
    some = count - own
    return pl.pallas_call(
        functools.partial(others_kernel, own, count),
        out_shape=(
            pltpu.VMEM((some, points, length), F32),
            pltpu.VMEM((3, length // LANES, rows, LANES), F32),
        ),
        in_specs=[smem] * 2 + [vmem] * 5,
        out_specs=[vmem, vmem],
        scratch_shapes=[pltpu.VMEM((some * points, 2 * length), BF16)] * 2,
        compiler_params=pltpu.CompilerParams(vmem_limit_bytes=12 * 1024 * 1024),
        cost_estimate=pl.CostEstimate(flops=1, bytes_accessed=1, transcendentals=0),
    )(scale, group, *map(in_vmem, (pred, correlation, khat, table, inverse)))


def adjoint_own(rhat, khat, inverse, vectors, weight, halos, own):
    count, points, length = vectors.shape
    vmem = pl.BlockSpec(memory_space=pltpu.VMEM)
    operands = (rhat, khat, inverse, vectors, weight, *halos)
    return pl.pallas_call(
        functools.partial(own_kernel, count),
        out_shape=pltpu.VMEM((own, points, length), F32),
        in_specs=[vmem] * len(operands),
        out_specs=vmem,
        scratch_shapes=[pltpu.VMEM((own * points, 2 * length), BF16)] * 2,
        compiler_params=pltpu.CompilerParams(vmem_limit_bytes=12 * 1024 * 1024),
        cost_estimate=pl.CostEstimate(
            flops=6 * own * points * length * length * 2, bytes_accessed=4 * khat.size, transcendentals=0
        ),
    )(*map(in_vmem, operands))


def ready_kernel(halo, corr_ref, stiff_ref, coup_ref, near_ref, out_ref, weight_ref):
    groups, length, _ = corr_ref.shape
    for g in range(groups):
        lanes = slice(g * length, (g + 1) * length)
        out_ref[:length, lanes], out_ref[length:, lanes] = split(corr_ref[g].T)

    place_here = lax.axis_index("pts")
    points = weight_ref.shape[1]
    span = weight_ref.shape[2]
    place = lax.broadcasted_iota(jnp.int32, (span, points), 0)
    here = lax.broadcasted_iota(jnp.int32, (span, points), 1) + halo
    coup = coup_ref[...]
    diagonal = stiff_ref[...] + jnp.sum(coup, axis=0, keepdims=True)
    weight = jnp.where(place == here, diagonal, 0.0)
    near = near_ref[...] - (place_here * points - halo)
    swap = (1 - place_here % 2) * (points + halo)
    near = near + jnp.where(near < halo, swap, 0) - jnp.where(near >= points + halo, swap, 0)
    for j in range(coup.shape[0]):
        weight = weight - jnp.where(place == near[j : j + 1], coup[j : j + 1], 0.0)
    weight_ref[0], weight_ref[1] = split(weight.T)


def ready(correlation, stiffness, couplings, neighbors):
    groups, length, _ = correlation.shape
    points = stiffness.shape[0]
    vmem = pl.BlockSpec(memory_space=pltpu.VMEM)
    return pl.pallas_call(
        functools.partial(ready_kernel, COLS),
        out_shape=(
            pltpu.VMEM((2 * length, groups * length), BF16),
            pltpu.VMEM((2, points, points + 2 * COLS), BF16),
        ),
        in_specs=[vmem] * 4,
        out_specs=[vmem] * 2,
        compiler_params=pltpu.CompilerParams(vmem_limit_bytes=8 * 1024 * 1024),
    )(*map(in_vmem, (correlation, stiffness[None], couplings, neighbors)))


def add_kernel(*refs):
    total = refs[0][...]
    for ref in refs[1:-1]:
        total = total + ref[...]
    refs[-1][...] = total


def add(*parts):
    vmem = pl.BlockSpec(memory_space=pltpu.VMEM)
    return pl.pallas_call(
        add_kernel,
        out_shape=jax.ShapeDtypeStruct(parts[0].shape, F32),
        in_specs=[vmem] * len(parts),
        out_specs=vmem,
        compiler_params=pltpu.CompilerParams(vmem_limit_bytes=4 * 1024 * 1024),
    )(*map(in_vmem, parts))


def stages(size):
    bits = [1 << bit for bit in range(size.bit_length() - 1)]
    masks = []
    while bits:
        low, *bits = bits
        masks.append([low])
        if bits:
            high, *bits = bits
            masks[-1] += [high, low + high]
    turned = list(masks)
    if len(masks) > 1 and len(masks[0]) == len(masks[1]):
        turned[0], turned[1] = masks[1], masks[0]
    return masks, turned


def local(table, inverse, kernel, vectors, noise_scale, sensor_group, correlation, stiffness, couplings, neighbors):
    sensors, points, length = kernel.shape
    count = vectors.shape[0]
    n_sens, n_pts = lax.axis_size("sens"), lax.axis_size("pts")
    own = count // n_sens

    pred, khat, table, inverse, vectors, correlation, *edges = forward(
        kernel, vectors, table, inverse, correlation, own
    )
    correlation, weight = ready(correlation, stiffness, couplings, neighbors)

    links = [[], []]
    for s in range(n_sens):
        for p in range(n_pts - 1):
            here = s * n_pts + p
            links[p % 2] += [(here, here + 1), (here + 1, here)]
        if n_sens % 2 == 0:
            for p in (0, n_pts - 1):
                links[1].append((s * n_pts + p, (s ^ 1) * n_pts + p))
    halos = []
    for step, (even, odd) in enumerate(zip(*stages(n_pts))):
        more = []
        for mask_even, mask_odd in zip(even, odd):
            pairs = [
                (s * n_pts + p, s * n_pts + (p ^ (mask_odd if s % 2 else mask_even)))
                for s in range(n_sens)
                for p in range(n_pts)
            ]
            more.append(lax.ppermute(pred, ("sens", "pts"), pairs))
        if step < 2:
            halos.append(lax.ppermute(edges[step], ("sens", "pts"), links[step]))
        for part in more:
            pred = pred + part
        if step == 0:
            pred, halos[0], correlation, edges[1] = lax.optimization_barrier(
                (pred, halos[0], correlation, edges[1])
            )

    rest, rhat = adjoint_others(pred, noise_scale, sensor_group, correlation, khat, table, inverse, own, count)
    rest, halos[1] = lax.optimization_barrier((rest, halos[1]))
    received = []
    for j in range(1, n_sens):
        pairs = [(s, (s + j) % n_sens) for s in range(n_sens)]
        received.append(lax.ppermute(rest[(j - 1) * own : j * own], "sens", pairs))
    total = adjoint_own(rhat, khat, inverse, vectors, weight, halos, own)
    return add(total, *received)


def solution(mesh):
    in_specs = (
        P(),
        P(),
        P("sens", "pts", None),
        P(None, "pts", None),
        P("sens"),
        P("sens"),
        P(),
        P("pts"),
        P(None, "pts"),
        P(None, "pts"),
    )
    out_specs = P("sens", "pts", None)
    mapped = jax.shard_map(local, mesh=mesh, in_specs=in_specs, out_specs=out_specs, check_vma=False)

    def run(kernel, *rest):
        tables = map(jnp.asarray, dft_tables(kernel.shape[-1]))
        return mapped(*tables, kernel, *rest)

    return run
```

```python
import functools
import math

import jax
import jax.numpy as jnp
import ml_dtypes
import numpy as np
from jax import lax
from jax.experimental import pallas as pl
from jax.experimental.pallas import tpu as pltpu
from jax.sharding import PartitionSpec as P

COLS = 16
ORDER = ((1, 2, 0), (1, 0, 2))
LANES = 128
SUB = 8
F32 = jnp.float32
BF16 = jnp.bfloat16


def halves_table(table):
    high = table.astype(ml_dtypes.bfloat16)
    low = (table - high.astype(np.float64)).astype(ml_dtypes.bfloat16)
    return np.concatenate([high, low], axis=0)


def dft_tables(length):
    steps = np.arange(length, dtype=np.int64)
    phase = (steps[:, None] * (2 * steps[None, :] + 1)) % (4 * length)
    angle = phase.astype(np.float64) * (2.0 * math.pi / (4 * length))
    pair = np.stack([np.cos(angle), -np.sin(angle)], axis=1)
    pair = pair.reshape(length, 2, length // LANES, LANES)
    table = pair.transpose(0, 2, 1, 3).reshape(length, 2 * length)
    return halves_table(table), halves_table(table.T)


def split(x):
    high = x.astype(BF16)
    return high, (x - high.astype(F32)).astype(BF16)


def dot(a, b):
    return jnp.dot(a, b, preferred_element_type=F32)


def in_vmem(x):
    return pltpu.with_memory_space_constraint(x, pltpu.VMEM)


def in_hbm(x):
    return pltpu.with_memory_space_constraint(x, pltpu.HBM)


def rows_at(start, size):
    return pl.ds(pl.multiple_of(start, size), size)


def sums(parts):
    row = lax.broadcasted_iota(jnp.int32, parts[0].shape, 0)
    width = 1
    while len(parts) > 1:
        first = row // width % 2 == 0
        parts = [
            jnp.where(first, a, b) + pltpu.roll(jnp.where(first, b, a), width, 0)
            for a, b in zip(parts[::2], parts[1::2])
        ]
        width *= 2
    return parts[0]


def back(high_ref, low_ref, inverse_ref):
    half = inverse_ref.shape[0] // 2
    high, low = high_ref[...], low_ref[...]
    upper, lower = inverse_ref[:half], inverse_ref[half:]
    return dot(high, upper) + dot(high, lower) + dot(low, upper)


def forward_kernel(
    kern_hbm,
    vec_hbm,
    table_hbm,
    inverse_hbm,
    corr_hbm,
    pred_ref,
    khat_ref,
    table_ref,
    inverse_ref,
    vec_ref,
    corr_ref,
    edge_ref,
    kern_ref,
    vhat_ref,
    kern_high_ref,
    kern_low_ref,
    vec_high_ref,
    vec_low_ref,
    high_ref,
    low_ref,
    sems,
):
    sensors, points, length = kern_ref.shape
    count = vec_ref.shape[0]
    both, halo, _ = edge_ref.shape
    sens = lax.axis_index("sens")
    shift = sens * (both // 2)
    upper_edge = (lax.axis_index("pts") + sens + 1) % 2
    cols = length // LANES
    kern_halves, vec_halves = (kern_high_ref, kern_low_ref), (vec_high_ref, vec_low_ref)

    pairs = [(kern_hbm, kern_ref), (vec_hbm, vec_ref)]
    for col in range(cols):
        lanes = slice(2 * col * LANES, 2 * (col + 1) * LANES)
        pairs.append((table_hbm.at[:, lanes], table_ref.at[:, lanes]))
    pairs.append((inverse_hbm, inverse_ref))
    pairs.append((corr_hbm, corr_ref))
    copies = [
        pltpu.make_async_copy(source, target, sems.at[i]) for i, (source, target) in enumerate(pairs)
    ]
    for i in (0, 2, 1, *range(3, len(copies))):
        copies[i].start()

    def fill(source_ref, halves, first):
        for i in range(source_ref.shape[0]):
            rows = slice(i * points, (i + 1) * points)
            value = source_ref[i if first is None else lax.rem(i + first, source_ref.shape[0])]
            halves[0][rows], halves[1][rows] = split(value)

    def transform(halves, col):
        high, low = halves[0][...], halves[1][...]
        lanes = slice(2 * col * LANES, 2 * (col + 1) * LANES)
        upper, lower = table_ref[:length, lanes], table_ref[length:, lanes]
        hat = dot(
            jnp.concatenate([high, high, low], axis=1), jnp.concatenate([upper, lower, upper], axis=0)
        )
        return hat[:, :LANES], hat[:, LANES:]

    def kern_column(col):
        real, imag = transform(kern_halves, col)
        khat_ref[0, col] = real
        khat_ref[1, col] = imag - real
        khat_ref[2, col] = imag + real

    def vec_column(col):
        real, imag = transform(vec_halves, col)
        vhat_ref[0, col] = real + imag
        vhat_ref[1, col] = real
        vhat_ref[2, col] = imag

    def product(col):
        rows = []
        for s in range(sensors):
            acc = [[None] * 3 for _ in range(count)]
            for g in range(points // SUB):
                at = s * points + g * SUB
                right = [khat_ref[c, col, at : at + SUB] for c in range(3)]
                for k in range(count):
                    for c in range(3):
                        at = k * points + g * SUB
                        term = vhat_ref[c, col, at : at + SUB] * right[c]
                        acc[k][c] = term if acc[k][c] is None else acc[k][c] + term
            real = sums([one - three for one, _, three in acc])
            imag = sums([one + two for one, two, _ in acc])
            rows.append(jnp.concatenate([real, imag], axis=1))
        lanes = slice(2 * col * LANES, 2 * (col + 1) * LANES)
        high_ref[:, lanes], low_ref[:, lanes] = split(jnp.concatenate(rows, axis=0))

    copies[0].wait()
    fill(kern_ref, kern_halves, None)
    copies[2].wait()
    kern_column(0)
    copies[1].wait()
    fill(vec_ref, vec_halves, shift)
    edge = rows_at(upper_edge * (points - halo), halo)
    for k in range(both):
        edge_ref[k] = vec_ref[sens // 2 * both + k, edge]
    for copy in copies[3:-1]:
        copy.wait()
    vec_column(0)
    for col in range(cols):
        if col + 1 < cols:
            kern_column(col + 1)
            vec_column(col + 1)
        product(col)
    pred_ref[...] = back(high_ref, low_ref, inverse_ref)
    copies[-1].wait()


def forward(kernel, vectors, table, inverse, correlation, own):
    sensors, points, length = kernel.shape
    count = vectors.shape[0]
    cols = length // LANES
    hbm = pl.BlockSpec(memory_space=pltpu.HBM)
    return pl.pallas_call(
        forward_kernel,
        out_shape=(
            pltpu.VMEM((sensors * count, length), F32),
            pltpu.VMEM((3, cols, sensors * points, LANES), F32),
            pltpu.VMEM((2 * length, 2 * length), BF16),
            pltpu.VMEM((4 * length, length), BF16),
            pltpu.VMEM(vectors.shape, F32),
            pltpu.VMEM(correlation.shape, F32),
            pltpu.VMEM((2 * own, COLS, length), F32),
        ),
        in_specs=[hbm] * 5,
        out_specs=[pl.BlockSpec(memory_space=pltpu.VMEM)] * 7,
        scratch_shapes=[
            pltpu.VMEM(kernel.shape, F32),
            pltpu.VMEM((3, cols, count * points, LANES), F32),
            pltpu.VMEM((sensors * points, length), BF16),
            pltpu.VMEM((sensors * points, length), BF16),
            pltpu.VMEM((count * points, length), BF16),
            pltpu.VMEM((count * points, length), BF16),
            pltpu.VMEM((sensors * count, 2 * length), BF16),
            pltpu.VMEM((sensors * count, 2 * length), BF16),
            pltpu.SemaphoreType.DMA((4 + cols,)),
        ],
        compiler_params=pltpu.CompilerParams(vmem_limit_bytes=14 * 1024 * 1024),
    )(*map(in_hbm, (kernel, vectors, table, inverse, correlation)))


def correlate(first, count, rhat_ref, khat_ref, inverse_ref, high_ref, low_ref, data_ref):
    some, points, length = data_ref.shape
    sensors = rhat_ref.shape[2] // count
    cols = length // LANES
    k_block, g_block = 4, 2
    tall = g_block * SUB

    def product(col, g0, ks):
        acc = {}
        for s in range(sensors):
            right = [
                [
                    khat_ref[c, col, pl.ds(s * points + g0 * tall + b * SUB, SUB)]
                    for c in range(3)
                ]
                for b in range(g_block)
            ]
            for k in ks:
                for c in range(3):
                    at = s * count + first + k
                    left = jnp.broadcast_to(rhat_ref[c, col, at : at + 1], (SUB, LANES))
                    for b in range(g_block):
                        term = left * right[b][c]
                        acc[k, b, c] = term if s == 0 else acc[k, b, c] + term
        for k in ks:
            re = jnp.concatenate([acc[k, b, 0] + acc[k, b, 1] for b in range(g_block)], axis=0)
            im = jnp.concatenate([acc[k, b, 0] - acc[k, b, 2] for b in range(g_block)], axis=0)
            at = slice(k * points + g0 * tall, k * points + (g0 + 1) * tall)
            lanes = slice(2 * col * LANES, (2 * col + 1) * LANES)
            others = slice((2 * col + 1) * LANES, (2 * col + 2) * LANES)
            high_ref[at, lanes], low_ref[at, lanes] = split(re)
            high_ref[at, others], low_ref[at, others] = split(im)

    for col in range(cols):
        for g0 in range(points // tall):
            for k0 in range(0, some, k_block):
                product(col, g0, range(k0, min(k0 + k_block, some)))
        lanes = slice(2 * col * LANES, 2 * (col + 1) * LANES)
        upper = inverse_ref[lanes]
        lower = inverse_ref[lanes.start + 2 * length : lanes.stop + 2 * length]
        high, low = high_ref[:, lanes], low_ref[:, lanes]
        part = dot(high, upper) + dot(high, lower) + dot(low, upper)
        part = part.reshape(some, points, length)
        data_ref[...] = data_ref[...] + part if col else part


def others_kernel(
    own,
    count,
    scale_ref,
    group_ref,
    pred_ref,
    corr_ref,
    khat_ref,
    table_ref,
    inverse_ref,
    rest_ref,
    rhat_ref,
    high_ref,
    low_ref,
):
    sensors = scale_ref.shape[0]
    length = pred_ref.shape[1]
    groups = corr_ref.shape[1] // length
    pred = pred_ref[...]
    high, low = split(pred)
    upper, lower = corr_ref[:length], corr_ref[length:]
    mixed = dot(
        jnp.concatenate([high, high, low], axis=1), jnp.concatenate([upper, lower, upper], axis=0)
    )
    whole = []
    for s in range(sensors):
        at = slice(s * count, (s + 1) * count)
        value = pred[at]
        for g in range(groups):
            weight = jnp.where(group_ref[s] == g, 1.0, 0.0)
            value = value + weight * mixed[at, g * length : (g + 1) * length]
        whole.append(value * (scale_ref[s] * (1.0 / (length * length))))
    high, low = split(jnp.concatenate(whole, axis=0))
    upper, lower = table_ref[:length], table_ref[length:]
    hat = dot(
        jnp.concatenate([high, high, low], axis=1), jnp.concatenate([upper, lower, upper], axis=0)
    )
    for col in range(length // LANES):
        real = hat[:, 2 * col * LANES : (2 * col + 1) * LANES]
        imag = hat[:, (2 * col + 1) * LANES : (2 * col + 2) * LANES]
        rhat_ref[0, col] = real + imag
        rhat_ref[1, col] = imag
        rhat_ref[2, col] = real
    correlate(own, count, rhat_ref, khat_ref, inverse_ref, high_ref, low_ref, rest_ref)


def own_kernel(
    count,
    rhat_ref,
    khat_ref,
    inverse_ref,
    vec_ref,
    weight_ref,
    mine_ref,
    other_ref,
    out_ref,
    high_ref,
    low_ref,
):
    correlate(0, count, rhat_ref, khat_ref, inverse_ref, high_ref, low_ref, out_ref)
    own = out_ref.shape[0]
    sens = lax.axis_index("sens")
    upper, lower = weight_ref[0], weight_ref[1]
    for k in range(own):
        here = vec_ref[lax.rem(sens * own + k, count)]
        mine, other = mine_ref[sens % 2 * own + k], other_ref[sens % 2 * own + k]
        first = jnp.where(sens % 2 == 0, mine, other)
        second = jnp.where(sens % 2 == 0, other, mine)
        value = jnp.concatenate([first, here, second], axis=0)
        high, low = split(value)
        out_ref[k] = out_ref[k] + dot(upper, high) + dot(upper, low) + dot(lower, high)


def adjoint_others(pred, scale, group, correlation, khat, table, inverse, own, count):
    rows, length = pred.shape
    points = khat.shape[2] // (rows // count)
    vmem = pl.BlockSpec(memory_space=pltpu.VMEM)
    smem = pl.BlockSpec(memory_space=pltpu.SMEM)
    some = count - own
    return pl.pallas_call(
        functools.partial(others_kernel, own, count),
        out_shape=(
            pltpu.VMEM((some, points, length), F32),
            pltpu.VMEM((3, length // LANES, rows, LANES), F32),
        ),
        in_specs=[smem] * 2 + [vmem] * 5,
        out_specs=[vmem, vmem],
        scratch_shapes=[pltpu.VMEM((some * points, 2 * length), BF16)] * 2,
        compiler_params=pltpu.CompilerParams(vmem_limit_bytes=12 * 1024 * 1024),
        cost_estimate=pl.CostEstimate(flops=1, bytes_accessed=1, transcendentals=0),
    )(scale, group, *map(in_vmem, (pred, correlation, khat, table, inverse)))


def adjoint_own(rhat, khat, inverse, vectors, weight, halos, own):
    count, points, length = vectors.shape
    vmem = pl.BlockSpec(memory_space=pltpu.VMEM)
    operands = (rhat, khat, inverse, vectors, weight, *halos)
    return pl.pallas_call(
        functools.partial(own_kernel, count),
        out_shape=pltpu.VMEM((own, points, length), F32),
        in_specs=[vmem] * len(operands),
        out_specs=vmem,
        scratch_shapes=[pltpu.VMEM((own * points, 2 * length), BF16)] * 2,
        compiler_params=pltpu.CompilerParams(vmem_limit_bytes=12 * 1024 * 1024),
        cost_estimate=pl.CostEstimate(
            flops=6 * own * points * length * length * 2, bytes_accessed=4 * khat.size, transcendentals=0
        ),
    )(*map(in_vmem, operands))


def ready_kernel(halo, corr_ref, stiff_ref, coup_ref, near_ref, out_ref, weight_ref):
    groups, length, _ = corr_ref.shape
    for g in range(groups):
        lanes = slice(g * length, (g + 1) * length)
        out_ref[:length, lanes], out_ref[length:, lanes] = split(corr_ref[g].T)

    place_here = lax.axis_index("pts")
    points = weight_ref.shape[1]
    span = weight_ref.shape[2]
    place = lax.broadcasted_iota(jnp.int32, (span, points), 0)
    here = lax.broadcasted_iota(jnp.int32, (span, points), 1) + halo
    coup = coup_ref[...]
    diagonal = stiff_ref[...] + jnp.sum(coup, axis=0, keepdims=True)
    weight = jnp.where(place == here, diagonal, 0.0)
    near = near_ref[...] - (place_here * points - halo)
    swap = (1 - place_here % 2) * (points + halo)
    near = near + jnp.where(near < halo, swap, 0) - jnp.where(near >= points + halo, swap, 0)
    for j in range(coup.shape[0]):
        weight = weight - jnp.where(place == near[j : j + 1], coup[j : j + 1], 0.0)
    weight_ref[0], weight_ref[1] = split(weight.T)


def ready(correlation, stiffness, couplings, neighbors):
    groups, length, _ = correlation.shape
    points = stiffness.shape[0]
    vmem = pl.BlockSpec(memory_space=pltpu.VMEM)
    return pl.pallas_call(
        functools.partial(ready_kernel, COLS),
        out_shape=(
            pltpu.VMEM((2 * length, groups * length), BF16),
            pltpu.VMEM((2, points, points + 2 * COLS), BF16),
        ),
        in_specs=[vmem] * 4,
        out_specs=[vmem] * 2,
        compiler_params=pltpu.CompilerParams(vmem_limit_bytes=8 * 1024 * 1024),
    )(*map(in_vmem, (correlation, stiffness[None], couplings, neighbors)))


def add_kernel(*refs):
    total = refs[0][...]
    for ref in refs[1:-1]:
        total = total + ref[...]
    refs[-1][...] = total


def add(*parts):
    vmem = pl.BlockSpec(memory_space=pltpu.VMEM)
    return pl.pallas_call(
        add_kernel,
        out_shape=jax.ShapeDtypeStruct(parts[0].shape, F32),
        in_specs=[vmem] * len(parts),
        out_specs=vmem,
        compiler_params=pltpu.CompilerParams(vmem_limit_bytes=4 * 1024 * 1024),
    )(*map(in_vmem, parts))


def stages(size):
    bits = [1 << bit for bit in range(size.bit_length() - 1)]
    masks = []
    while bits:
        low, *bits = bits
        masks.append([low])
        if bits:
            high, *bits = bits
            both = [low, high, low + high]
            masks[-1] = [both[i] for i in (ORDER[1] if len(masks) > 1 else ORDER[0])]
    turned = list(masks)
    if len(masks) > 1 and len(masks[0]) == len(masks[1]):
        turned[0], turned[1] = masks[1], masks[0]
    return masks, turned


def local(table, inverse, kernel, vectors, noise_scale, sensor_group, correlation, stiffness, couplings, neighbors):
    sensors, points, length = kernel.shape
    count = vectors.shape[0]
    n_sens, n_pts = lax.axis_size("sens"), lax.axis_size("pts")
    own = count // n_sens

    pred, khat, table, inverse, vectors, correlation, edge = forward(
        kernel, vectors, table, inverse, correlation, own
    )
    correlation, weight = ready(correlation, stiffness, couplings, neighbors)

    links = []
    for s in range(n_sens):
        for p in range(n_pts):
            partner = p ^ 1 if s % 2 == 0 else ((p - 1) ^ 1) + 1
            links.append((s * n_pts + p, s * n_pts + partner % n_pts))
    across = [(s, s ^ 1) for s in range(n_sens)]
    halos = []
    for step, (even, odd) in enumerate(zip(*stages(n_pts))):
        more = []
        for mask_even, mask_odd in zip(even, odd):
            pairs = [
                (s * n_pts + p, s * n_pts + (p ^ (mask_odd if s % 2 else mask_even)))
                for s in range(n_sens)
                for p in range(n_pts)
            ]
            more.append(lax.ppermute(pred, ("sens", "pts"), pairs))
        if step == 0:
            halos.append(lax.ppermute(edge, ("sens", "pts"), links))
        for part in more:
            pred = pred + part
        if step == 0:
            pred, correlation = lax.optimization_barrier((pred, correlation))
            halos.append(lax.ppermute(halos[0], "sens", across))
    pred, halos[1] = lax.optimization_barrier((pred, halos[1]))

    rest, rhat = adjoint_others(pred, noise_scale, sensor_group, correlation, khat, table, inverse, own, count)
    received = []
    for j in range(1, n_sens):
        pairs = [(s, (s + j) % n_sens) for s in range(n_sens)]
        received.append(lax.ppermute(rest[(j - 1) * own : j * own], "sens", pairs))
    total = adjoint_own(rhat, khat, inverse, vectors, weight, halos, own)
    return add(total, *received)


def solution(mesh):
    in_specs = (
        P(),
        P(),
        P("sens", "pts", None),
        P(None, "pts", None),
        P("sens"),
        P("sens"),
        P(),
        P("pts"),
        P(None, "pts"),
        P(None, "pts"),
    )
    out_specs = P("sens", "pts", None)
    mapped = jax.shard_map(local, mesh=mesh, in_specs=in_specs, out_specs=out_specs, check_vma=False)

    def run(kernel, *rest):
        tables = map(jnp.asarray, dft_tables(kernel.shape[-1]))
        return mapped(*tables, kernel, *rest)

    return run
```

```python
import functools
import math

import jax
import jax.numpy as jnp
import ml_dtypes
import numpy as np
from jax import lax
from jax.experimental import pallas as pl
from jax.experimental.pallas import tpu as pltpu
from jax.sharding import PartitionSpec as P

COLS = 16
ORDER = ((1, 0, 2), (0, 1, 2))
LANES = 128
SUB = 8
F32 = jnp.float32
BF16 = jnp.bfloat16


def halves_table(table):
    high = table.astype(ml_dtypes.bfloat16)
    low = (table - high.astype(np.float64)).astype(ml_dtypes.bfloat16)
    return np.concatenate([high, low], axis=0)


def dft_tables(length):
    steps = np.arange(length, dtype=np.int64)
    phase = (steps[:, None] * (2 * steps[None, :] + 1)) % (4 * length)
    angle = phase.astype(np.float64) * (2.0 * math.pi / (4 * length))
    pair = np.stack([np.cos(angle), -np.sin(angle)], axis=1)
    pair = pair.reshape(length, 2, length // LANES, LANES)
    table = pair.transpose(0, 2, 1, 3).reshape(length, 2 * length)
    return halves_table(table), halves_table(table.T)


def split(x):
    high = x.astype(BF16)
    return high, (x - high.astype(F32)).astype(BF16)


def dot(a, b):
    return jnp.dot(a, b, preferred_element_type=F32)


def in_vmem(x):
    return pltpu.with_memory_space_constraint(x, pltpu.VMEM)


def in_hbm(x):
    return pltpu.with_memory_space_constraint(x, pltpu.HBM)


def rows_at(start, size):
    return pl.ds(pl.multiple_of(start, size), size)


def sums(parts):
    row = lax.broadcasted_iota(jnp.int32, parts[0].shape, 0)
    width = 1
    while len(parts) > 1:
        first = row // width % 2 == 0
        parts = [
            jnp.where(first, a, b) + pltpu.roll(jnp.where(first, b, a), width, 0)
            for a, b in zip(parts[::2], parts[1::2])
        ]
        width *= 2
    return parts[0]


def back(high_ref, low_ref, inverse_ref):
    half = inverse_ref.shape[0] // 2
    high, low = high_ref[...], low_ref[...]
    upper, lower = inverse_ref[:half], inverse_ref[half:]
    return dot(high, upper) + dot(high, lower) + dot(low, upper)


def forward_kernel(
    kern_hbm,
    vec_hbm,
    table_hbm,
    inverse_hbm,
    corr_hbm,
    pred_ref,
    khat_ref,
    table_ref,
    inverse_ref,
    vec_ref,
    corr_ref,
    edge_ref,
    kern_ref,
    vhat_ref,
    kern_high_ref,
    kern_low_ref,
    vec_high_ref,
    vec_low_ref,
    high_ref,
    low_ref,
    sems,
):
    sensors, points, length = kern_ref.shape
    count = vec_ref.shape[0]
    both, halo, _ = edge_ref.shape
    sens = lax.axis_index("sens")
    shift = sens * (both // 2)
    upper_edge = (lax.axis_index("pts") + sens + 1) % 2
    cols = length // LANES
    kern_halves, vec_halves = (kern_high_ref, kern_low_ref), (vec_high_ref, vec_low_ref)

    pairs = [(kern_hbm, kern_ref), (vec_hbm, vec_ref)]
    for col in range(cols):
        lanes = slice(2 * col * LANES, 2 * (col + 1) * LANES)
        pairs.append((table_hbm.at[:, lanes], table_ref.at[:, lanes]))
    pairs.append((inverse_hbm, inverse_ref))
    pairs.append((corr_hbm, corr_ref))
    copies = [
        pltpu.make_async_copy(source, target, sems.at[i]) for i, (source, target) in enumerate(pairs)
    ]
    for i in (0, 2, 1, *range(3, len(copies))):
        copies[i].start()

    def fill(source_ref, halves, first):
        for i in range(source_ref.shape[0]):
            rows = slice(i * points, (i + 1) * points)
            value = source_ref[i if first is None else lax.rem(i + first, source_ref.shape[0])]
            halves[0][rows], halves[1][rows] = split(value)

    def transform(halves, col):
        high, low = halves[0][...], halves[1][...]
        lanes = slice(2 * col * LANES, 2 * (col + 1) * LANES)
        upper, lower = table_ref[:length, lanes], table_ref[length:, lanes]
        hat = dot(
            jnp.concatenate([high, high, low], axis=1), jnp.concatenate([upper, lower, upper], axis=0)
        )
        return hat[:, :LANES], hat[:, LANES:]

    def kern_column(col):
        real, imag = transform(kern_halves, col)
        khat_ref[0, col] = real
        khat_ref[1, col] = imag - real
        khat_ref[2, col] = imag + real

    def vec_column(col):
        real, imag = transform(vec_halves, col)
        vhat_ref[0, col] = real + imag
        vhat_ref[1, col] = real
        vhat_ref[2, col] = imag

    def product(col):
        rows = []
        for s in range(sensors):
            acc = [[None] * 3 for _ in range(count)]
            for g in range(points // SUB):
                at = s * points + g * SUB
                right = [khat_ref[c, col, at : at + SUB] for c in range(3)]
                for k in range(count):
                    for c in range(3):
                        at = k * points + g * SUB
                        term = vhat_ref[c, col, at : at + SUB] * right[c]
                        acc[k][c] = term if acc[k][c] is None else acc[k][c] + term
            real = sums([one - three for one, _, three in acc])
            imag = sums([one + two for one, two, _ in acc])
            rows.append(jnp.concatenate([real, imag], axis=1))
        lanes = slice(2 * col * LANES, 2 * (col + 1) * LANES)
        high_ref[:, lanes], low_ref[:, lanes] = split(jnp.concatenate(rows, axis=0))

    copies[0].wait()
    fill(kern_ref, kern_halves, None)
    copies[2].wait()
    kern_column(0)
    copies[1].wait()
    fill(vec_ref, vec_halves, shift)
    edge = rows_at(upper_edge * (points - halo), halo)
    for k in range(both):
        edge_ref[k] = vec_ref[sens // 2 * both + k, edge]
    for copy in copies[3:-1]:
        copy.wait()
    vec_column(0)
    for col in range(cols):
        if col + 1 < cols:
            kern_column(col + 1)
            vec_column(col + 1)
        product(col)
    pred_ref[...] = back(high_ref, low_ref, inverse_ref)
    copies[-1].wait()


def forward(kernel, vectors, table, inverse, correlation, own):
    sensors, points, length = kernel.shape
    count = vectors.shape[0]
    cols = length // LANES
    hbm = pl.BlockSpec(memory_space=pltpu.HBM)
    return pl.pallas_call(
        forward_kernel,
        out_shape=(
            pltpu.VMEM((sensors * count, length), F32),
            pltpu.VMEM((3, cols, sensors * points, LANES), F32),
            pltpu.VMEM((2 * length, 2 * length), BF16),
            pltpu.VMEM((4 * length, length), BF16),
            pltpu.VMEM(vectors.shape, F32),
            pltpu.VMEM(correlation.shape, F32),
            pltpu.VMEM((2 * own, COLS, length), F32),
        ),
        in_specs=[hbm] * 5,
        out_specs=[pl.BlockSpec(memory_space=pltpu.VMEM)] * 7,
        scratch_shapes=[
            pltpu.VMEM(kernel.shape, F32),
            pltpu.VMEM((3, cols, count * points, LANES), F32),
            pltpu.VMEM((sensors * points, length), BF16),
            pltpu.VMEM((sensors * points, length), BF16),
            pltpu.VMEM((count * points, length), BF16),
            pltpu.VMEM((count * points, length), BF16),
            pltpu.VMEM((sensors * count, 2 * length), BF16),
            pltpu.VMEM((sensors * count, 2 * length), BF16),
            pltpu.SemaphoreType.DMA((4 + cols,)),
        ],
        compiler_params=pltpu.CompilerParams(vmem_limit_bytes=14 * 1024 * 1024),
    )(*map(in_hbm, (kernel, vectors, table, inverse, correlation)))


def correlate(first, count, rhat_ref, khat_ref, inverse_ref, high_ref, low_ref, data_ref):
    some, points, length = data_ref.shape
    sensors = rhat_ref.shape[2] // count
    cols = length // LANES
    k_block, g_block = 4, 2
    tall = g_block * SUB

    def product(col, g0, ks):
        acc = {}
        for s in range(sensors):
            right = [
                [
                    khat_ref[c, col, pl.ds(s * points + g0 * tall + b * SUB, SUB)]
                    for c in range(3)
                ]
                for b in range(g_block)
            ]
            for k in ks:
                for c in range(3):
                    at = s * count + first + k
                    left = jnp.broadcast_to(rhat_ref[c, col, at : at + 1], (SUB, LANES))
                    for b in range(g_block):
                        term = left * right[b][c]
                        acc[k, b, c] = term if s == 0 else acc[k, b, c] + term
        for k in ks:
            re = jnp.concatenate([acc[k, b, 0] + acc[k, b, 1] for b in range(g_block)], axis=0)
            im = jnp.concatenate([acc[k, b, 0] - acc[k, b, 2] for b in range(g_block)], axis=0)
            at = slice(k * points + g0 * tall, k * points + (g0 + 1) * tall)
            lanes = slice(2 * col * LANES, (2 * col + 1) * LANES)
            others = slice((2 * col + 1) * LANES, (2 * col + 2) * LANES)
            high_ref[at, lanes], low_ref[at, lanes] = split(re)
            high_ref[at, others], low_ref[at, others] = split(im)

    for col in range(cols):
        for g0 in range(points // tall):
            for k0 in range(0, some, k_block):
                product(col, g0, range(k0, min(k0 + k_block, some)))
        lanes = slice(2 * col * LANES, 2 * (col + 1) * LANES)
        upper = inverse_ref[lanes]
        lower = inverse_ref[lanes.start + 2 * length : lanes.stop + 2 * length]
        high, low = high_ref[:, lanes], low_ref[:, lanes]
        part = dot(high, upper) + dot(high, lower) + dot(low, upper)
        part = part.reshape(some, points, length)
        data_ref[...] = data_ref[...] + part if col else part


def others_kernel(
    own,
    count,
    scale_ref,
    group_ref,
    pred_ref,
    corr_ref,
    khat_ref,
    table_ref,
    inverse_ref,
    rest_ref,
    rhat_ref,
    high_ref,
    low_ref,
):
    sensors = scale_ref.shape[0]
    length = pred_ref.shape[1]
    groups = corr_ref.shape[1] // length
    pred = pred_ref[...]
    high, low = split(pred)
    upper, lower = corr_ref[:length], corr_ref[length:]
    mixed = dot(
        jnp.concatenate([high, high, low], axis=1), jnp.concatenate([upper, lower, upper], axis=0)
    )
    whole = []
    for s in range(sensors):
        at = slice(s * count, (s + 1) * count)
        value = pred[at]
        for g in range(groups):
            weight = jnp.where(group_ref[s] == g, 1.0, 0.0)
            value = value + weight * mixed[at, g * length : (g + 1) * length]
        whole.append(value * (scale_ref[s] * (1.0 / (length * length))))
    high, low = split(jnp.concatenate(whole, axis=0))
    upper, lower = table_ref[:length], table_ref[length:]
    hat = dot(
        jnp.concatenate([high, high, low], axis=1), jnp.concatenate([upper, lower, upper], axis=0)
    )
    for col in range(length // LANES):
        real = hat[:, 2 * col * LANES : (2 * col + 1) * LANES]
        imag = hat[:, (2 * col + 1) * LANES : (2 * col + 2) * LANES]
        rhat_ref[0, col] = real + imag
        rhat_ref[1, col] = imag
        rhat_ref[2, col] = real
    correlate(own, count, rhat_ref, khat_ref, inverse_ref, high_ref, low_ref, rest_ref)


def own_kernel(
    count,
    rhat_ref,
    khat_ref,
    inverse_ref,
    vec_ref,
    weight_ref,
    mine_ref,
    other_ref,
    out_ref,
    high_ref,
    low_ref,
):
    correlate(0, count, rhat_ref, khat_ref, inverse_ref, high_ref, low_ref, out_ref)
    own = out_ref.shape[0]
    sens = lax.axis_index("sens")
    weight = weight_ref[...]
    for k in range(own):
        here = vec_ref[lax.rem(sens * own + k, count)]
        mine, other = mine_ref[sens % 2 * own + k], other_ref[sens % 2 * own + k]
        first = jnp.where(sens % 2 == 0, mine, other)
        second = jnp.where(sens % 2 == 0, other, mine)
        value = jnp.concatenate([first, here, second], axis=0)
        high, low = split(value)
        out_ref[k] = out_ref[k] + dot(weight, jnp.concatenate([high, low, high], axis=0))


def adjoint_others(pred, scale, group, correlation, khat, table, inverse, own, count):
    rows, length = pred.shape
    points = khat.shape[2] // (rows // count)
    vmem = pl.BlockSpec(memory_space=pltpu.VMEM)
    smem = pl.BlockSpec(memory_space=pltpu.SMEM)
    some = count - own
    return pl.pallas_call(
        functools.partial(others_kernel, own, count),
        out_shape=(
            pltpu.VMEM((some, points, length), F32),
            pltpu.VMEM((3, length // LANES, rows, LANES), F32),
        ),
        in_specs=[smem] * 2 + [vmem] * 5,
        out_specs=[vmem, vmem],
        scratch_shapes=[pltpu.VMEM((some * points, 2 * length), BF16)] * 2,
        compiler_params=pltpu.CompilerParams(vmem_limit_bytes=12 * 1024 * 1024),
        cost_estimate=pl.CostEstimate(flops=1, bytes_accessed=1, transcendentals=0),
    )(scale, group, *map(in_vmem, (pred, correlation, khat, table, inverse)))


def adjoint_own(rhat, khat, inverse, vectors, weight, halos, own):
    count, points, length = vectors.shape
    vmem = pl.BlockSpec(memory_space=pltpu.VMEM)
    operands = (rhat, khat, inverse, vectors, weight, *halos)
    return pl.pallas_call(
        functools.partial(own_kernel, count),
        out_shape=pltpu.VMEM((own, points, length), F32),
        in_specs=[vmem] * len(operands),
        out_specs=vmem,
        scratch_shapes=[pltpu.VMEM((own * points, 2 * length), BF16)] * 2,
        compiler_params=pltpu.CompilerParams(vmem_limit_bytes=12 * 1024 * 1024),
        cost_estimate=pl.CostEstimate(
            flops=6 * own * points * length * length * 2, bytes_accessed=4 * khat.size, transcendentals=0
        ),
    )(*map(in_vmem, operands))


def ready_kernel(halo, corr_ref, stiff_ref, coup_ref, near_ref, out_ref, weight_ref):
    groups, length, _ = corr_ref.shape
    for g in range(groups):
        lanes = slice(g * length, (g + 1) * length)
        out_ref[:length, lanes], out_ref[length:, lanes] = split(corr_ref[g].T)

    place_here = lax.axis_index("pts")
    points = weight_ref.shape[0]
    span = points + 2 * halo
    place = lax.broadcasted_iota(jnp.int32, (span, points), 0)
    here = lax.broadcasted_iota(jnp.int32, (span, points), 1) + halo
    coup = coup_ref[...]
    diagonal = stiff_ref[...] + jnp.sum(coup, axis=0, keepdims=True)
    weight = jnp.where(place == here, diagonal, 0.0)
    near = near_ref[...] - (place_here * points - halo)
    swap = (1 - place_here % 2) * (points + halo)
    near = near + jnp.where(near < halo, swap, 0) - jnp.where(near >= points + halo, swap, 0)
    for j in range(coup.shape[0]):
        weight = weight - jnp.where(place == near[j : j + 1], coup[j : j + 1], 0.0)
    high, low = split(weight.T)
    for i, part in enumerate((high, high, low)):
        weight_ref[:, i * span : (i + 1) * span] = part


def ready(correlation, stiffness, couplings, neighbors):
    groups, length, _ = correlation.shape
    points = stiffness.shape[0]
    vmem = pl.BlockSpec(memory_space=pltpu.VMEM)
    return pl.pallas_call(
        functools.partial(ready_kernel, COLS),
        out_shape=(
            pltpu.VMEM((2 * length, groups * length), BF16),
            pltpu.VMEM((points, 3 * (points + 2 * COLS)), BF16),
        ),
        in_specs=[vmem] * 4,
        out_specs=[vmem] * 2,
        compiler_params=pltpu.CompilerParams(vmem_limit_bytes=8 * 1024 * 1024),
    )(*map(in_vmem, (correlation, stiffness[None], couplings, neighbors)))


def add_kernel(*refs):
    total = refs[0][...]
    for ref in refs[1:-1]:
        total = total + ref[...]
    refs[-1][...] = total


def add(*parts):
    vmem = pl.BlockSpec(memory_space=pltpu.VMEM)
    return pl.pallas_call(
        add_kernel,
        out_shape=jax.ShapeDtypeStruct(parts[0].shape, F32),
        in_specs=[vmem] * len(parts),
        out_specs=vmem,
        compiler_params=pltpu.CompilerParams(vmem_limit_bytes=4 * 1024 * 1024),
    )(*map(in_vmem, parts))


def stages(size):
    bits = [1 << bit for bit in range(size.bit_length() - 1)]
    masks = []
    while bits:
        low, *bits = bits
        masks.append([low])
        if bits:
            high, *bits = bits
            both = [low, high, low + high]
            masks[-1] = [both[i] for i in (ORDER[1] if len(masks) > 1 else ORDER[0])]
    turned = list(masks)
    if len(masks) > 1 and len(masks[0]) == len(masks[1]):
        turned[0], turned[1] = masks[1], masks[0]
    return masks, turned


def local(table, inverse, kernel, vectors, noise_scale, sensor_group, correlation, stiffness, couplings, neighbors):
    sensors, points, length = kernel.shape
    count = vectors.shape[0]
    n_sens, n_pts = lax.axis_size("sens"), lax.axis_size("pts")
    own = count // n_sens

    pred, khat, table, inverse, vectors, correlation, edge = forward(
        kernel, vectors, table, inverse, correlation, own
    )
    correlation, weight = ready(correlation, stiffness, couplings, neighbors)

    links = []
    for s in range(n_sens):
        for p in range(n_pts):
            partner = p ^ 1 if s % 2 == 0 else ((p - 1) ^ 1) + 1
            links.append((s * n_pts + p, s * n_pts + partner % n_pts))
    across = [(s, s ^ 1) for s in range(n_sens)]
    halos = []
    for step, (even, odd) in enumerate(zip(*stages(n_pts))):
        more = []
        for mask_even, mask_odd in zip(even, odd):
            pairs = [
                (s * n_pts + p, s * n_pts + (p ^ (mask_odd if s % 2 else mask_even)))
                for s in range(n_sens)
                for p in range(n_pts)
            ]
            more.append(lax.ppermute(pred, ("sens", "pts"), pairs))
        if step == 0:
            halos.append(lax.ppermute(edge, ("sens", "pts"), links))
        for part in more:
            pred = pred + part
        if step == 0:
            pred, correlation = lax.optimization_barrier((pred, correlation))
            halos.append(lax.ppermute(halos[0], "sens", across))
    pred, halos[1] = lax.optimization_barrier((pred, halos[1]))

    rest, rhat = adjoint_others(pred, noise_scale, sensor_group, correlation, khat, table, inverse, own, count)
    received = []
    for j in range(1, n_sens):
        pairs = [(s, (s + j) % n_sens) for s in range(n_sens)]
        received.append(lax.ppermute(rest[(j - 1) * own : j * own], "sens", pairs))
    total = adjoint_own(rhat, khat, inverse, vectors, weight, halos, own)
    return add(total, *received)


def solution(mesh):
    in_specs = (
        P(),
        P(),
        P("sens", "pts", None),
        P(None, "pts", None),
        P("sens"),
        P("sens"),
        P(),
        P("pts"),
        P(None, "pts"),
        P(None, "pts"),
    )
    out_specs = P("sens", "pts", None)
    mapped = jax.shard_map(local, mesh=mesh, in_specs=in_specs, out_specs=out_specs, check_vma=False)

    def run(kernel, *rest):
        tables = map(jnp.asarray, dft_tables(kernel.shape[-1]))
        return mapped(*tables, kernel, *rest)

    return run
```

```python
import functools
import math

import jax
import jax.numpy as jnp
import ml_dtypes
import numpy as np
from jax import lax
from jax.experimental import pallas as pl
from jax.experimental.pallas import tpu as pltpu
from jax.sharding import PartitionSpec as P

COLS = 16
LANES = 128
SUB = 8
F32 = jnp.float32
BF16 = jnp.bfloat16


def halves_table(table):
    high = table.astype(ml_dtypes.bfloat16)
    low = (table - high.astype(np.float64)).astype(ml_dtypes.bfloat16)
    return np.concatenate([high, low], axis=0)


def dft_tables(length):
    steps = np.arange(length, dtype=np.int64)
    phase = (steps[:, None] * (2 * steps[None, :] + 1)) % (4 * length)
    angle = phase.astype(np.float64) * (2.0 * math.pi / (4 * length))
    pair = np.stack([np.cos(angle), -np.sin(angle)], axis=1)
    pair = pair.reshape(length, 2, length // LANES, LANES)
    table = pair.transpose(0, 2, 1, 3).reshape(length, 2 * length)
    return halves_table(table), halves_table(table.T)


def split(x):
    high = x.astype(BF16)
    return high, (x - high.astype(F32)).astype(BF16)


def dot(a, b):
    return jnp.dot(a, b, preferred_element_type=F32)


def in_vmem(x):
    return pltpu.with_memory_space_constraint(x, pltpu.VMEM)


def in_hbm(x):
    return pltpu.with_memory_space_constraint(x, pltpu.HBM)


def rows_at(start, size):
    return pl.ds(pl.multiple_of(start, size), size)


def sums(parts):
    row = lax.broadcasted_iota(jnp.int32, parts[0].shape, 0)
    width = 1
    while len(parts) > 1:
        first = row // width % 2 == 0
        parts = [
            jnp.where(first, a, b) + pltpu.roll(jnp.where(first, b, a), width, 0)
            for a, b in zip(parts[::2], parts[1::2])
        ]
        width *= 2
    return parts[0]


def back(high_ref, low_ref, inverse_ref):
    half = inverse_ref.shape[0] // 2
    high, low = high_ref[...], low_ref[...]
    upper, lower = inverse_ref[:half], inverse_ref[half:]
    return dot(high, upper) + dot(high, lower) + dot(low, upper)


def forward_kernel(
    kern_hbm,
    vec_hbm,
    table_hbm,
    inverse_hbm,
    corr_hbm,
    pred_ref,
    khat_ref,
    table_ref,
    inverse_ref,
    vec_ref,
    corr_ref,
    edge_ref,
    kern_ref,
    vhat_ref,
    kern_high_ref,
    kern_low_ref,
    vec_high_ref,
    vec_low_ref,
    high_ref,
    low_ref,
    sems,
):
    sensors, points, length = kern_ref.shape
    count = vec_ref.shape[0]
    both, halo, _ = edge_ref.shape
    sens = lax.axis_index("sens")
    shift = sens * (both // 2)
    upper_edge = (lax.axis_index("pts") + sens + 1) % 2
    cols = length // LANES
    kern_halves, vec_halves = (kern_high_ref, kern_low_ref), (vec_high_ref, vec_low_ref)

    pairs = [(kern_hbm, kern_ref), (vec_hbm, vec_ref)]
    for col in range(cols):
        lanes = slice(2 * col * LANES, 2 * (col + 1) * LANES)
        pairs.append((table_hbm.at[:, lanes], table_ref.at[:, lanes]))
    pairs.append((inverse_hbm, inverse_ref))
    pairs.append((corr_hbm, corr_ref))
    copies = [
        pltpu.make_async_copy(source, target, sems.at[i]) for i, (source, target) in enumerate(pairs)
    ]
    for i in (0, 2, 1, *range(3, len(copies))):
        copies[i].start()

    def fill(source_ref, halves, first):
        for i in range(source_ref.shape[0]):
            rows = slice(i * points, (i + 1) * points)
            value = source_ref[i if first is None else lax.rem(i + first, source_ref.shape[0])]
            halves[0][rows], halves[1][rows] = split(value)

    def transform(halves, col):
        high, low = halves[0][...], halves[1][...]
        lanes = slice(2 * col * LANES, 2 * (col + 1) * LANES)
        upper, lower = table_ref[:length, lanes], table_ref[length:, lanes]
        hat = dot(
            jnp.concatenate([high, high, low], axis=1), jnp.concatenate([upper, lower, upper], axis=0)
        )
        return hat[:, :LANES], hat[:, LANES:]

    def kern_column(col):
        real, imag = transform(kern_halves, col)
        khat_ref[0, col] = real
        khat_ref[1, col] = imag - real
        khat_ref[2, col] = imag + real

    def vec_column(col):
        real, imag = transform(vec_halves, col)
        vhat_ref[0, col] = real + imag
        vhat_ref[1, col] = real
        vhat_ref[2, col] = imag

    def product(col):
        rows = []
        for s in range(sensors):
            acc = [[None] * 3 for _ in range(count)]
            for g in range(points // SUB):
                at = s * points + g * SUB
                right = [khat_ref[c, col, at : at + SUB] for c in range(3)]
                for k in range(count):
                    for c in range(3):
                        at = k * points + g * SUB
                        term = vhat_ref[c, col, at : at + SUB] * right[c]
                        acc[k][c] = term if acc[k][c] is None else acc[k][c] + term
            real = sums([one - three for one, _, three in acc])
            imag = sums([one + two for one, two, _ in acc])
            rows.append(jnp.concatenate([real, imag], axis=1))
        lanes = slice(2 * col * LANES, 2 * (col + 1) * LANES)
        high_ref[:, lanes], low_ref[:, lanes] = split(jnp.concatenate(rows, axis=0))

    copies[0].wait()
    fill(kern_ref, kern_halves, None)
    copies[2].wait()
    kern_column(0)
    copies[1].wait()
    fill(vec_ref, vec_halves, shift)
    edge = rows_at(upper_edge * (points - halo), halo)
    for k in range(both):
        edge_ref[k] = vec_ref[sens // 2 * both + k, edge]
    for copy in copies[3:-1]:
        copy.wait()
    vec_column(0)
    for col in range(cols):
        if col + 1 < cols:
            kern_column(col + 1)
            vec_column(col + 1)
        product(col)
    pred_ref[...] = back(high_ref, low_ref, inverse_ref)
    copies[-1].wait()


def forward(kernel, vectors, table, inverse, correlation, own):
    sensors, points, length = kernel.shape
    count = vectors.shape[0]
    cols = length // LANES
    hbm = pl.BlockSpec(memory_space=pltpu.HBM)
    return pl.pallas_call(
        forward_kernel,
        out_shape=(
            pltpu.VMEM((sensors * count, length), F32),
            pltpu.VMEM((3, cols, sensors * points, LANES), F32),
            pltpu.VMEM((2 * length, 2 * length), BF16),
            pltpu.VMEM((4 * length, length), BF16),
            pltpu.VMEM(vectors.shape, F32),
            pltpu.VMEM(correlation.shape, F32),
            pltpu.VMEM((2 * own, COLS, length), F32),
        ),
        in_specs=[hbm] * 5,
        out_specs=[pl.BlockSpec(memory_space=pltpu.VMEM)] * 7,
        scratch_shapes=[
            pltpu.VMEM(kernel.shape, F32),
            pltpu.VMEM((3, cols, count * points, LANES), F32),
            pltpu.VMEM((sensors * points, length), BF16),
            pltpu.VMEM((sensors * points, length), BF16),
            pltpu.VMEM((count * points, length), BF16),
            pltpu.VMEM((count * points, length), BF16),
            pltpu.VMEM((sensors * count, 2 * length), BF16),
            pltpu.VMEM((sensors * count, 2 * length), BF16),
            pltpu.SemaphoreType.DMA((4 + cols,)),
        ],
        compiler_params=pltpu.CompilerParams(vmem_limit_bytes=14 * 1024 * 1024),
    )(*map(in_hbm, (kernel, vectors, table, inverse, correlation)))


def correlate(first, count, rhat_ref, khat_ref, inverse_ref, high_ref, low_ref, data_ref):
    some, points, length = data_ref.shape
    sensors = rhat_ref.shape[2] // count
    cols = length // LANES
    k_block, g_block = 4, 2
    tall = g_block * SUB

    def product(col, g0, ks):
        acc = {}
        for s in range(sensors):
            right = [
                [
                    khat_ref[c, col, pl.ds(s * points + g0 * tall + b * SUB, SUB)]
                    for c in range(3)
                ]
                for b in range(g_block)
            ]
            for k in ks:
                for c in range(3):
                    at = s * count + first + k
                    left = jnp.broadcast_to(rhat_ref[c, col, at : at + 1], (SUB, LANES))
                    for b in range(g_block):
                        term = left * right[b][c]
                        acc[k, b, c] = term if s == 0 else acc[k, b, c] + term
        for k in ks:
            re = jnp.concatenate([acc[k, b, 0] + acc[k, b, 1] for b in range(g_block)], axis=0)
            im = jnp.concatenate([acc[k, b, 0] - acc[k, b, 2] for b in range(g_block)], axis=0)
            at = slice(k * points + g0 * tall, k * points + (g0 + 1) * tall)
            lanes = slice(2 * col * LANES, (2 * col + 1) * LANES)
            others = slice((2 * col + 1) * LANES, (2 * col + 2) * LANES)
            high_ref[at, lanes], low_ref[at, lanes] = split(re)
            high_ref[at, others], low_ref[at, others] = split(im)

    for col in range(cols):
        for g0 in range(points // tall):
            for k0 in range(0, some, k_block):
                product(col, g0, range(k0, min(k0 + k_block, some)))
        lanes = slice(2 * col * LANES, 2 * (col + 1) * LANES)
        upper = inverse_ref[lanes]
        lower = inverse_ref[lanes.start + 2 * length : lanes.stop + 2 * length]
        high, low = high_ref[:, lanes], low_ref[:, lanes]
        part = dot(high, upper) + dot(high, lower) + dot(low, upper)
        part = part.reshape(some, points, length)
        data_ref[...] = data_ref[...] + part if col else part


def others_kernel(
    own,
    count,
    pred_ref,
    corr_ref,
    pick_ref,
    khat_ref,
    table_ref,
    inverse_ref,
    rest_ref,
    rhat_ref,
    high_ref,
    low_ref,
):
    length = pred_ref.shape[1]
    groups = corr_ref.shape[1] // length
    times = length // LANES

    def rowwise(g):
        return jnp.concatenate([pick_ref[g]] * times, axis=1)

    pred = pred_ref[...]
    high, low = split(pred)
    lhs = jnp.concatenate([high, high, low], axis=1)
    whole = rowwise(groups) * pred
    for g in range(groups):
        lanes = slice(g * length, (g + 1) * length)
        upper, lower = corr_ref[:length, lanes], corr_ref[length:, lanes]
        whole = whole + rowwise(g) * dot(lhs, jnp.concatenate([upper, lower, upper], axis=0))
    high, low = split(whole)
    upper, lower = table_ref[:length], table_ref[length:]
    hat = dot(
        jnp.concatenate([high, high, low], axis=1), jnp.concatenate([upper, lower, upper], axis=0)
    )
    for col in range(length // LANES):
        real = hat[:, 2 * col * LANES : (2 * col + 1) * LANES]
        imag = hat[:, (2 * col + 1) * LANES : (2 * col + 2) * LANES]
        rhat_ref[0, col] = real + imag
        rhat_ref[1, col] = imag
        rhat_ref[2, col] = real
    correlate(own, count, rhat_ref, khat_ref, inverse_ref, high_ref, low_ref, rest_ref)


def own_kernel(
    count,
    rhat_ref,
    khat_ref,
    inverse_ref,
    vec_ref,
    weight_ref,
    mine_ref,
    other_ref,
    out_ref,
    high_ref,
    low_ref,
):
    correlate(0, count, rhat_ref, khat_ref, inverse_ref, high_ref, low_ref, out_ref)
    own = out_ref.shape[0]
    sens = lax.axis_index("sens")
    weight = weight_ref[...]
    for k in range(own):
        here = vec_ref[lax.rem(sens * own + k, count)]
        mine, other = mine_ref[sens % 2 * own + k], other_ref[sens % 2 * own + k]
        first = jnp.where(sens % 2 == 0, mine, other)
        second = jnp.where(sens % 2 == 0, other, mine)
        value = jnp.concatenate([first, here, second], axis=0)
        high, low = split(value)
        out_ref[k] = out_ref[k] + dot(weight, jnp.concatenate([high, low, high], axis=0))


def adjoint_others(pred, correlation, pick, khat, table, inverse, own, count):
    rows, length = pred.shape
    points = khat.shape[2] // (rows // count)
    vmem = pl.BlockSpec(memory_space=pltpu.VMEM)
    some = count - own
    return pl.pallas_call(
        functools.partial(others_kernel, own, count),
        out_shape=(
            pltpu.VMEM((some, points, length), F32),
            pltpu.VMEM((3, length // LANES, rows, LANES), F32),
        ),
        in_specs=[vmem] * 6,
        out_specs=[vmem, vmem],
        scratch_shapes=[pltpu.VMEM((some * points, 2 * length), BF16)] * 2,
        compiler_params=pltpu.CompilerParams(vmem_limit_bytes=12 * 1024 * 1024),
        cost_estimate=pl.CostEstimate(flops=1, bytes_accessed=1, transcendentals=0),
    )(*map(in_vmem, (pred, correlation, pick, khat, table, inverse)))


def adjoint_own(rhat, khat, inverse, vectors, weight, halos, own):
    count, points, length = vectors.shape
    vmem = pl.BlockSpec(memory_space=pltpu.VMEM)
    operands = (rhat, khat, inverse, vectors, weight, *halos)
    return pl.pallas_call(
        functools.partial(own_kernel, count),
        out_shape=pltpu.VMEM((own, points, length), F32),
        in_specs=[vmem] * len(operands),
        out_specs=vmem,
        scratch_shapes=[pltpu.VMEM((own * points, 2 * length), BF16)] * 2,
        compiler_params=pltpu.CompilerParams(vmem_limit_bytes=12 * 1024 * 1024),
        cost_estimate=pl.CostEstimate(
            flops=6 * own * points * length * length * 2, bytes_accessed=4 * khat.size, transcendentals=0
        ),
    )(*map(in_vmem, operands))


def ready_kernel(
    halo, scale_ref, group_ref, corr_ref, stiff_ref, coup_ref, near_ref, out_ref, pick_ref, weight_ref
):
    groups, length, _ = corr_ref.shape
    sensors = scale_ref.shape[0]
    sensor = lax.broadcasted_iota(jnp.int32, pick_ref.shape[1:], 0) // (pick_ref.shape[1] // sensors)
    factor = jnp.zeros(sensor.shape, F32)
    member = jnp.zeros(sensor.shape, jnp.int32)
    for s in range(sensors):
        factor = jnp.where(sensor == s, scale_ref[s], factor)
        member = jnp.where(sensor == s, group_ref[s], member)
    factor = factor * (1.0 / (length * length))
    for g in range(groups):
        pick_ref[g] = jnp.where(member == g, factor, 0.0)
    pick_ref[groups] = factor

    for g in range(groups):
        lanes = slice(g * length, (g + 1) * length)
        out_ref[:length, lanes], out_ref[length:, lanes] = split(corr_ref[g].T)

    place_here = lax.axis_index("pts")
    points = weight_ref.shape[0]
    span = points + 2 * halo
    place = lax.broadcasted_iota(jnp.int32, (span, points), 0)
    here = lax.broadcasted_iota(jnp.int32, (span, points), 1) + halo
    coup = coup_ref[...]
    diagonal = stiff_ref[...] + jnp.sum(coup, axis=0, keepdims=True)
    weight = jnp.where(place == here, diagonal, 0.0)
    near = near_ref[...] - (place_here * points - halo)
    swap = (1 - place_here % 2) * (points + halo)
    near = near + jnp.where(near < halo, swap, 0) - jnp.where(near >= points + halo, swap, 0)
    for j in range(coup.shape[0]):
        weight = weight - jnp.where(place == near[j : j + 1], coup[j : j + 1], 0.0)
    high, low = split(weight.T)
    for i, part in enumerate((high, high, low)):
        weight_ref[:, i * span : (i + 1) * span] = part


def ready(rows, scale, group, correlation, stiffness, couplings, neighbors):
    groups, length, _ = correlation.shape
    points = stiffness.shape[0]
    vmem = pl.BlockSpec(memory_space=pltpu.VMEM)
    smem = pl.BlockSpec(memory_space=pltpu.SMEM)
    return pl.pallas_call(
        functools.partial(ready_kernel, COLS),
        out_shape=(
            pltpu.VMEM((2 * length, groups * length), BF16),
            pltpu.VMEM((groups + 1, rows, LANES), F32),
            pltpu.VMEM((points, 3 * (points + 2 * COLS)), BF16),
        ),
        in_specs=[smem] * 2 + [vmem] * 4,
        out_specs=[vmem] * 3,
        compiler_params=pltpu.CompilerParams(vmem_limit_bytes=8 * 1024 * 1024),
    )(scale, group, *map(in_vmem, (correlation, stiffness[None], couplings, neighbors)))


def add_kernel(*refs):
    total = refs[0][...]
    for ref in refs[1:-1]:
        total = total + ref[...]
    refs[-1][...] = total


def add(*parts):
    vmem = pl.BlockSpec(memory_space=pltpu.VMEM)
    return pl.pallas_call(
        add_kernel,
        out_shape=jax.ShapeDtypeStruct(parts[0].shape, F32),
        in_specs=[vmem] * len(parts),
        out_specs=vmem,
        compiler_params=pltpu.CompilerParams(vmem_limit_bytes=4 * 1024 * 1024),
    )(*map(in_vmem, parts))


def stages(size):
    bits = [1 << bit for bit in range(size.bit_length() - 1)]
    masks = []
    while bits:
        low, *bits = bits
        masks.append([low])
        if bits:
            high, *bits = bits
            masks[-1] = [low + high, low, high]
    turned = list(masks)
    if len(masks) > 1 and len(masks[0]) == len(masks[1]):
        turned[0], turned[1] = masks[1], masks[0]
    return masks, turned


def local(table, inverse, kernel, vectors, noise_scale, sensor_group, correlation, stiffness, couplings, neighbors):
    sensors, points, length = kernel.shape
    count = vectors.shape[0]
    n_sens, n_pts = lax.axis_size("sens"), lax.axis_size("pts")
    own = count // n_sens

    pred, khat, table, inverse, vectors, correlation, edge = forward(
        kernel, vectors, table, inverse, correlation, own
    )
    correlation, pick, weight = ready(
        pred.shape[0], noise_scale, sensor_group, correlation, stiffness, couplings, neighbors
    )

    links = []
    for s in range(n_sens):
        for p in range(n_pts):
            partner = p ^ 1 if s % 2 == 0 else ((p - 1) ^ 1) + 1
            links.append((s * n_pts + p, s * n_pts + partner % n_pts))
    across = [(s, s ^ 1) for s in range(n_sens)]
    halos = []
    for step, (even, odd) in enumerate(zip(*stages(n_pts))):
        more = []
        for mask_even, mask_odd in zip(even, odd):
            pairs = [
                (s * n_pts + p, s * n_pts + (p ^ (mask_odd if s % 2 else mask_even)))
                for s in range(n_sens)
                for p in range(n_pts)
            ]
            more.append(lax.ppermute(pred, ("sens", "pts"), pairs))
        if step == 0:
            halos.append(lax.ppermute(edge, ("sens", "pts"), links))
        for part in more:
            pred = pred + part
        if step == 0:
            pred, correlation = lax.optimization_barrier((pred, correlation))
            halos.append(lax.ppermute(halos[0], "sens", across))
    pred, halos[1] = lax.optimization_barrier((pred, halos[1]))

    rest, rhat = adjoint_others(pred, correlation, pick, khat, table, inverse, own, count)
    received = []
    for j in range(1, n_sens):
        pairs = [(s, (s + j) % n_sens) for s in range(n_sens)]
        received.append(lax.ppermute(rest[(j - 1) * own : j * own], "sens", pairs))
    total = adjoint_own(rhat, khat, inverse, vectors, weight, halos, own)
    return add(total, *received)


def solution(mesh):
    in_specs = (
        P(),
        P(),
        P("sens", "pts", None),
        P(None, "pts", None),
        P("sens"),
        P("sens"),
        P(),
        P("pts"),
        P(None, "pts"),
        P(None, "pts"),
    )
    out_specs = P("sens", "pts", None)
    mapped = jax.shard_map(local, mesh=mesh, in_specs=in_specs, out_specs=out_specs, check_vma=False)

    def run(kernel, *rest):
        tables = map(jnp.asarray, dft_tables(kernel.shape[-1]))
        return mapped(*tables, kernel, *rest)

    return run
```

```python
import functools
import math

import jax
import jax.numpy as jnp
import ml_dtypes
import numpy as np
from jax import lax
from jax.experimental import pallas as pl
from jax.experimental.pallas import tpu as pltpu
from jax.sharding import PartitionSpec as P

COLS = 16
LANES = 128
SUB = 8
F32 = jnp.float32
BF16 = jnp.bfloat16


def halves_table(table):
    high = table.astype(ml_dtypes.bfloat16)
    low = (table - high.astype(np.float64)).astype(ml_dtypes.bfloat16)
    return np.concatenate([high, low], axis=0)


def dft_tables(length):
    steps = np.arange(length, dtype=np.int64)
    phase = (steps[:, None] * (2 * steps[None, :] + 1)) % (4 * length)
    angle = phase.astype(np.float64) * (2.0 * math.pi / (4 * length))
    pair = np.stack([np.cos(angle), -np.sin(angle)], axis=1)
    pair = pair.reshape(length, 2, length // LANES, LANES)
    table = pair.transpose(0, 2, 1, 3).reshape(length, 2 * length)
    return halves_table(table), halves_table(table.T)


def split(x):
    high = x.astype(BF16)
    return high, (x - high.astype(F32)).astype(BF16)


def dot(a, b):
    return jnp.dot(a, b, preferred_element_type=F32)


def in_vmem(x):
    return pltpu.with_memory_space_constraint(x, pltpu.VMEM)


def in_hbm(x):
    return pltpu.with_memory_space_constraint(x, pltpu.HBM)


def rows_at(start, size):
    return pl.ds(pl.multiple_of(start, size), size)


def sums(parts):
    row = lax.broadcasted_iota(jnp.int32, parts[0].shape, 0)
    width = 1
    while len(parts) > 1:
        first = row // width % 2 == 0
        parts = [
            jnp.where(first, a, b) + pltpu.roll(jnp.where(first, b, a), width, 0)
            for a, b in zip(parts[::2], parts[1::2])
        ]
        width *= 2
    return parts[0]


def back(high_ref, low_ref, inverse_ref):
    half = inverse_ref.shape[0] // 2
    high, low = high_ref[...], low_ref[...]
    upper, lower = inverse_ref[:half], inverse_ref[half:]
    return dot(high, upper) + dot(high, lower) + dot(low, upper)


def forward_kernel(
    kern_hbm,
    vec_hbm,
    table_hbm,
    inverse_hbm,
    corr_hbm,
    pred_ref,
    khat_ref,
    table_ref,
    inverse_ref,
    vec_ref,
    corr_ref,
    edge_ref,
    kern_ref,
    vhat_ref,
    kern_high_ref,
    kern_low_ref,
    vec_high_ref,
    vec_low_ref,
    high_ref,
    low_ref,
    sems,
):
    sensors, points, length = kern_ref.shape
    count = vec_ref.shape[0]
    both, halo, _ = edge_ref.shape
    sens = lax.axis_index("sens")
    shift = sens * (both // 2)
    upper_edge = (lax.axis_index("pts") + sens + 1) % 2
    cols = length // LANES
    kern_halves, vec_halves = (kern_high_ref, kern_low_ref), (vec_high_ref, vec_low_ref)

    pairs = [(kern_hbm, kern_ref), (vec_hbm, vec_ref)]
    for col in range(cols):
        lanes = slice(2 * col * LANES, 2 * (col + 1) * LANES)
        pairs.append((table_hbm.at[:, lanes], table_ref.at[:, lanes]))
    pairs.append((inverse_hbm, inverse_ref))
    pairs.append((corr_hbm, corr_ref))
    copies = [
        pltpu.make_async_copy(source, target, sems.at[i]) for i, (source, target) in enumerate(pairs)
    ]
    for copy in copies:
        copy.start()

    def fill(source_ref, halves, first):
        for i in range(source_ref.shape[0]):
            rows = slice(i * points, (i + 1) * points)
            value = source_ref[i if first is None else lax.rem(i + first, source_ref.shape[0])]
            halves[0][rows], halves[1][rows] = split(value)

    def transform(halves, col):
        high, low = halves[0][...], halves[1][...]
        lanes = slice(2 * col * LANES, 2 * (col + 1) * LANES)
        upper, lower = table_ref[:length, lanes], table_ref[length:, lanes]
        hat = dot(
            jnp.concatenate([high, high, low], axis=1), jnp.concatenate([upper, lower, upper], axis=0)
        )
        return hat[:, :LANES], hat[:, LANES:]

    def kern_column(col):
        real, imag = transform(kern_halves, col)
        khat_ref[0, col] = real
        khat_ref[1, col] = imag - real
        khat_ref[2, col] = imag + real

    def vec_column(col):
        real, imag = transform(vec_halves, col)
        vhat_ref[0, col] = real + imag
        vhat_ref[1, col] = real
        vhat_ref[2, col] = imag

    def product(col):
        rows = []
        for s in range(sensors):
            acc = [[None] * 3 for _ in range(count)]
            for g in range(points // SUB):
                at = s * points + g * SUB
                right = [khat_ref[c, col, at : at + SUB] for c in range(3)]
                for k in range(count):
                    for c in range(3):
                        at = k * points + g * SUB
                        term = vhat_ref[c, col, at : at + SUB] * right[c]
                        acc[k][c] = term if acc[k][c] is None else acc[k][c] + term
            real = sums([one - three for one, _, three in acc])
            imag = sums([one + two for one, two, _ in acc])
            rows.append(jnp.concatenate([real, imag], axis=1))
        lanes = slice(2 * col * LANES, 2 * (col + 1) * LANES)
        high_ref[:, lanes], low_ref[:, lanes] = split(jnp.concatenate(rows, axis=0))

    copies[0].wait()
    fill(kern_ref, kern_halves, None)
    copies[2].wait()
    copies[1].wait()
    fill(vec_ref, vec_halves, shift)
    edge = rows_at(upper_edge * (points - halo), halo)
    for k in range(both):
        edge_ref[k] = vec_ref[sens // 2 * both + k, edge]
    for copy in copies[3:-1]:
        copy.wait()
    kern_column(0)
    vec_column(0)
    for col in range(cols):
        if col + 1 < cols:
            kern_column(col + 1)
            vec_column(col + 1)
        product(col)
    pred_ref[...] = back(high_ref, low_ref, inverse_ref)
    copies[-1].wait()


def forward(kernel, vectors, table, inverse, correlation, own):
    sensors, points, length = kernel.shape
    count = vectors.shape[0]
    cols = length // LANES
    hbm = pl.BlockSpec(memory_space=pltpu.HBM)
    return pl.pallas_call(
        forward_kernel,
        out_shape=(
            pltpu.VMEM((sensors * count, length), F32),
            pltpu.VMEM((3, cols, sensors * points, LANES), F32),
            pltpu.VMEM((2 * length, 2 * length), BF16),
            pltpu.VMEM((4 * length, length), BF16),
            pltpu.VMEM(vectors.shape, F32),
            pltpu.VMEM(correlation.shape, F32),
            pltpu.VMEM((2 * own, COLS, length), F32),
        ),
        in_specs=[hbm] * 5,
        out_specs=[pl.BlockSpec(memory_space=pltpu.VMEM)] * 7,
        scratch_shapes=[
            pltpu.VMEM(kernel.shape, F32),
            pltpu.VMEM((3, cols, count * points, LANES), F32),
            pltpu.VMEM((sensors * points, length), BF16),
            pltpu.VMEM((sensors * points, length), BF16),
            pltpu.VMEM((count * points, length), BF16),
            pltpu.VMEM((count * points, length), BF16),
            pltpu.VMEM((sensors * count, 2 * length), BF16),
            pltpu.VMEM((sensors * count, 2 * length), BF16),
            pltpu.SemaphoreType.DMA((4 + cols,)),
        ],
        compiler_params=pltpu.CompilerParams(vmem_limit_bytes=14 * 1024 * 1024),
    )(*map(in_hbm, (kernel, vectors, table, inverse, correlation)))


def correlate(first, count, rhat_ref, khat_ref, inverse_ref, high_ref, low_ref, data_ref):
    some, points, length = data_ref.shape
    sensors = rhat_ref.shape[2] // count
    cols = length // LANES
    k_block, g_block = 4, 2
    tall = g_block * SUB

    def product(col, g0, ks):
        acc = {}
        for s in range(sensors):
            right = [
                [
                    khat_ref[c, col, pl.ds(s * points + g0 * tall + b * SUB, SUB)]
                    for c in range(3)
                ]
                for b in range(g_block)
            ]
            for k in ks:
                for c in range(3):
                    at = s * count + first + k
                    left = jnp.broadcast_to(rhat_ref[c, col, at : at + 1], (SUB, LANES))
                    for b in range(g_block):
                        term = left * right[b][c]
                        acc[k, b, c] = term if s == 0 else acc[k, b, c] + term
        for k in ks:
            re = jnp.concatenate([acc[k, b, 0] + acc[k, b, 1] for b in range(g_block)], axis=0)
            im = jnp.concatenate([acc[k, b, 0] - acc[k, b, 2] for b in range(g_block)], axis=0)
            at = slice(k * points + g0 * tall, k * points + (g0 + 1) * tall)
            lanes = slice(2 * col * LANES, (2 * col + 1) * LANES)
            others = slice((2 * col + 1) * LANES, (2 * col + 2) * LANES)
            high_ref[at, lanes], low_ref[at, lanes] = split(re)
            high_ref[at, others], low_ref[at, others] = split(im)

    for col in range(cols):
        for g0 in range(points // tall):
            for k0 in range(0, some, k_block):
                product(col, g0, range(k0, min(k0 + k_block, some)))
        lanes = slice(2 * col * LANES, 2 * (col + 1) * LANES)
        upper = inverse_ref[lanes]
        lower = inverse_ref[lanes.start + 2 * length : lanes.stop + 2 * length]
        high, low = high_ref[:, lanes], low_ref[:, lanes]
        part = dot(high, upper) + dot(high, lower) + dot(low, upper)
        part = part.reshape(some, points, length)
        data_ref[...] = data_ref[...] + part if col else part


def others_kernel(
    own,
    count,
    pred_ref,
    corr_ref,
    pick_ref,
    khat_ref,
    table_ref,
    inverse_ref,
    rest_ref,
    rhat_ref,
    high_ref,
    low_ref,
):
    length = pred_ref.shape[1]
    groups = corr_ref.shape[1] // length
    times = length // LANES

    def rowwise(g):
        return jnp.concatenate([pick_ref[g]] * times, axis=1)

    pred = pred_ref[...]
    high, low = split(pred)
    lhs = jnp.concatenate([high, high, low], axis=1)
    whole = rowwise(groups) * pred
    for g in range(groups):
        lanes = slice(g * length, (g + 1) * length)
        upper, lower = corr_ref[:length, lanes], corr_ref[length:, lanes]
        whole = whole + rowwise(g) * dot(lhs, jnp.concatenate([upper, lower, upper], axis=0))
    high, low = split(whole)
    upper, lower = table_ref[:length], table_ref[length:]
    hat = dot(
        jnp.concatenate([high, high, low], axis=1), jnp.concatenate([upper, lower, upper], axis=0)
    )
    for col in range(length // LANES):
        real = hat[:, 2 * col * LANES : (2 * col + 1) * LANES]
        imag = hat[:, (2 * col + 1) * LANES : (2 * col + 2) * LANES]
        rhat_ref[0, col] = real + imag
        rhat_ref[1, col] = imag
        rhat_ref[2, col] = real
    correlate(own, count, rhat_ref, khat_ref, inverse_ref, high_ref, low_ref, rest_ref)


def own_kernel(
    count,
    rhat_ref,
    khat_ref,
    inverse_ref,
    vec_ref,
    weight_ref,
    mine_ref,
    other_ref,
    out_ref,
    high_ref,
    low_ref,
):
    correlate(0, count, rhat_ref, khat_ref, inverse_ref, high_ref, low_ref, out_ref)
    own = out_ref.shape[0]
    sens = lax.axis_index("sens")
    weight = weight_ref[...]
    for k in range(own):
        here = vec_ref[lax.rem(sens * own + k, count)]
        mine, other = mine_ref[sens % 2 * own + k], other_ref[sens % 2 * own + k]
        first = jnp.where(sens % 2 == 0, mine, other)
        second = jnp.where(sens % 2 == 0, other, mine)
        value = jnp.concatenate([first, here, second], axis=0)
        high, low = split(value)
        out_ref[k] = out_ref[k] + dot(weight, jnp.concatenate([high, low, high], axis=0))


def adjoint_others(pred, correlation, pick, khat, table, inverse, own, count):
    rows, length = pred.shape
    points = khat.shape[2] // (rows // count)
    vmem = pl.BlockSpec(memory_space=pltpu.VMEM)
    some = count - own
    return pl.pallas_call(
        functools.partial(others_kernel, own, count),
        out_shape=(
            pltpu.VMEM((some, points, length), F32),
            pltpu.VMEM((3, length // LANES, rows, LANES), F32),
        ),
        in_specs=[vmem] * 6,
        out_specs=[vmem, vmem],
        scratch_shapes=[pltpu.VMEM((some * points, 2 * length), BF16)] * 2,
        compiler_params=pltpu.CompilerParams(vmem_limit_bytes=12 * 1024 * 1024),
        cost_estimate=pl.CostEstimate(flops=1, bytes_accessed=1, transcendentals=0),
    )(*map(in_vmem, (pred, correlation, pick, khat, table, inverse)))


def adjoint_own(rhat, khat, inverse, vectors, weight, halos, own):
    count, points, length = vectors.shape
    vmem = pl.BlockSpec(memory_space=pltpu.VMEM)
    operands = (rhat, khat, inverse, vectors, weight, *halos)
    return pl.pallas_call(
        functools.partial(own_kernel, count),
        out_shape=pltpu.VMEM((own, points, length), F32),
        in_specs=[vmem] * len(operands),
        out_specs=vmem,
        scratch_shapes=[pltpu.VMEM((own * points, 2 * length), BF16)] * 2,
        compiler_params=pltpu.CompilerParams(vmem_limit_bytes=12 * 1024 * 1024),
        cost_estimate=pl.CostEstimate(
            flops=6 * own * points * length * length * 2, bytes_accessed=4 * khat.size, transcendentals=0
        ),
    )(*map(in_vmem, operands))


def ready_kernel(
    halo, scale_ref, group_ref, corr_ref, stiff_ref, coup_ref, near_ref, out_ref, pick_ref, weight_ref
):
    groups, length, _ = corr_ref.shape
    sensors = scale_ref.shape[0]
    sensor = lax.broadcasted_iota(jnp.int32, pick_ref.shape[1:], 0) // (pick_ref.shape[1] // sensors)
    factor = jnp.zeros(sensor.shape, F32)
    member = jnp.zeros(sensor.shape, jnp.int32)
    for s in range(sensors):
        factor = jnp.where(sensor == s, scale_ref[s], factor)
        member = jnp.where(sensor == s, group_ref[s], member)
    factor = factor * (1.0 / (length * length))
    for g in range(groups):
        pick_ref[g] = jnp.where(member == g, factor, 0.0)
    pick_ref[groups] = factor

    for g in range(groups):
        lanes = slice(g * length, (g + 1) * length)
        out_ref[:length, lanes], out_ref[length:, lanes] = split(corr_ref[g].T)

    place_here = lax.axis_index("pts")
    points = weight_ref.shape[0]
    span = points + 2 * halo
    place = lax.broadcasted_iota(jnp.int32, (span, points), 0)
    here = lax.broadcasted_iota(jnp.int32, (span, points), 1) + halo
    coup = coup_ref[...]
    diagonal = stiff_ref[...] + jnp.sum(coup, axis=0, keepdims=True)
    weight = jnp.where(place == here, diagonal, 0.0)
    near = near_ref[...] - (place_here * points - halo)
    swap = (1 - place_here % 2) * (points + halo)
    near = near + jnp.where(near < halo, swap, 0) - jnp.where(near >= points + halo, swap, 0)
    for j in range(coup.shape[0]):
        weight = weight - jnp.where(place == near[j : j + 1], coup[j : j + 1], 0.0)
    high, low = split(weight.T)
    for i, part in enumerate((high, high, low)):
        weight_ref[:, i * span : (i + 1) * span] = part


def ready(rows, scale, group, correlation, stiffness, couplings, neighbors):
    groups, length, _ = correlation.shape
    points = stiffness.shape[0]
    vmem = pl.BlockSpec(memory_space=pltpu.VMEM)
    smem = pl.BlockSpec(memory_space=pltpu.SMEM)
    return pl.pallas_call(
        functools.partial(ready_kernel, COLS),
        out_shape=(
            pltpu.VMEM((2 * length, groups * length), BF16),
            pltpu.VMEM((groups + 1, rows, LANES), F32),
            pltpu.VMEM((points, 3 * (points + 2 * COLS)), BF16),
        ),
        in_specs=[smem] * 2 + [vmem] * 4,
        out_specs=[vmem] * 3,
        compiler_params=pltpu.CompilerParams(vmem_limit_bytes=8 * 1024 * 1024),
    )(scale, group, *map(in_vmem, (correlation, stiffness[None], couplings, neighbors)))


def add_kernel(*refs):
    total = refs[0][...]
    for ref in refs[1:-1]:
        total = total + ref[...]
    refs[-1][...] = total


def add(*parts):
    vmem = pl.BlockSpec(memory_space=pltpu.VMEM)
    return pl.pallas_call(
        add_kernel,
        out_shape=jax.ShapeDtypeStruct(parts[0].shape, F32),
        in_specs=[vmem] * len(parts),
        out_specs=vmem,
        compiler_params=pltpu.CompilerParams(vmem_limit_bytes=4 * 1024 * 1024),
    )(*map(in_vmem, parts))


def stages(size):
    bits = [1 << bit for bit in range(size.bit_length() - 1)]
    masks = []
    while bits:
        low, *bits = bits
        masks.append([low])
        if bits:
            high, *bits = bits
            masks[-1] = [low + high, low, high]
    turned = list(masks)
    if len(masks) > 1 and len(masks[0]) == len(masks[1]):
        turned[0], turned[1] = masks[1], masks[0]
    return masks, turned


def local(table, inverse, kernel, vectors, noise_scale, sensor_group, correlation, stiffness, couplings, neighbors):
    sensors, points, length = kernel.shape
    count = vectors.shape[0]
    n_sens, n_pts = lax.axis_size("sens"), lax.axis_size("pts")
    own = count // n_sens

    pred, khat, table, inverse, vectors, correlation, edge = forward(
        kernel, vectors, table, inverse, correlation, own
    )
    correlation, pick, weight = ready(
        pred.shape[0], noise_scale, sensor_group, correlation, stiffness, couplings, neighbors
    )

    links = []
    for s in range(n_sens):
        for p in range(n_pts):
            partner = p ^ 1 if s % 2 == 0 else ((p - 1) ^ 1) + 1
            links.append((s * n_pts + p, s * n_pts + partner % n_pts))
    across = [(s, s ^ 1) for s in range(n_sens)]
    halos = []
    for step, (even, odd) in enumerate(zip(*stages(n_pts))):
        more = []
        for mask_even, mask_odd in zip(even, odd):
            pairs = [
                (s * n_pts + p, s * n_pts + (p ^ (mask_odd if s % 2 else mask_even)))
                for s in range(n_sens)
                for p in range(n_pts)
            ]
            more.append(lax.ppermute(pred, ("sens", "pts"), pairs))
        if step == 0:
            halos.append(lax.ppermute(edge, ("sens", "pts"), links))
        for part in more:
            pred = pred + part
        if step == 0:
            pred, correlation = lax.optimization_barrier((pred, correlation))
            halos.append(lax.ppermute(halos[0], "sens", across))
    pred, halos[1] = lax.optimization_barrier((pred, halos[1]))

    rest, rhat = adjoint_others(pred, correlation, pick, khat, table, inverse, own, count)
    received = []
    for j in range(1, n_sens):
        pairs = [(s, (s + j) % n_sens) for s in range(n_sens)]
        received.append(lax.ppermute(rest[(j - 1) * own : j * own], "sens", pairs))
    total = adjoint_own(rhat, khat, inverse, vectors, weight, halos, own)
    return add(total, *received)


def solution(mesh):
    in_specs = (
        P(),
        P(),
        P("sens", "pts", None),
        P(None, "pts", None),
        P("sens"),
        P("sens"),
        P(),
        P("pts"),
        P(None, "pts"),
        P(None, "pts"),
    )
    out_specs = P("sens", "pts", None)
    mapped = jax.shard_map(local, mesh=mesh, in_specs=in_specs, out_specs=out_specs, check_vma=False)

    def run(kernel, *rest):
        tables = map(jnp.asarray, dft_tables(kernel.shape[-1]))
        return mapped(*tables, kernel, *rest)

    return run
```
